256 devices in a mesh: pairs: 64 (over z, y, core), quad: 4 (over x).
Axes of the slice: x: 4, y: 4, z: 8, core: 2. Of those that a mesh axis runs over, the one named last changes fastest.
Arguments:
- picture_descriptors: bfloat16 [1024, 2048, 256], P('pairs', 'quad'), may hold values from -80 to 80
- image_slot: int32 [1024], replicated, may hold values from 0 to 1023, as said below
- group_images: int32 [640], P('pairs'), may hold values from 0 to 1023, as said below
- pair_target: int32 [128], P('pairs'), may hold values from 0 to 7
- pair_count: int32 [64], P('pairs'), may hold values from 1 to 2, 80 in all
Outputs:
- correspondence_result: float32 [128, 3, 2048], P('pairs', None, 'quad')
The draws below stay inside these ranges and needn't reach their ends.
Inputs may be any that keep to these rules, and one draw needn't show every extreme that they name: A permutation; image i is stored in row image_slot[i], on the devices of pairs index image_slot[i] div 16. `group_images`: entries g * 10 to g * 10 + 9 are the distinct images of group g, its 8 reference images first, then its 2 query images; at most 1 images of one group are stored on one pairs index, and in every group some pairs index stores exactly 1 of them. Group g uses its pairs 0 to pair_count[g] - 1.
All inputs are finite; a program needn't handle non-finite values.
Results may differ from the reference program's by a relative error of at most 0.00035.
Values may be sent and summed in bfloat16 or wider, within the bound.
No kernel may reach another device: no remote copies, remote signals or barrier semaphores. Data moves between devices by JAX's collectives and lax.ppermute only.
A program may use at most 128 MiB of HBM per device.

```python
import math
import jax
import jax.numpy as jnp
import numpy as np
from jax import lax

DESCRIPTOR_DEPTH = 256
IMG_W = 64
IMG_DEV = 16
PAIR_G = 2
TGT_G = 8
IMG_H = 32
TOKENS_IMG = 2048
IMAGES = 1024
GROUPS = 64
IMG_G = 10
CAP = 1
PAIRS = 128
N_PAIRS = 64


def ownership_tables(key):
    base = jax.random.fold_in(key, 7)
    perm_key, owner_key, first_key, second_key = jax.random.split(base, 4)
    image_slot = jax.random.permutation(perm_key, IMAGES).astype(jnp.int32)
    stored_image = jnp.zeros((IMAGES,), jnp.int32).at[image_slot].set(jnp.arange(IMAGES, dtype=jnp.int32))
    owner_keys = jax.random.split(owner_key, N_PAIRS)
    orders = jax.vmap(lambda single_key: jax.random.permutation(single_key, N_PAIRS))(owner_keys).astype(jnp.int32)
    group_member = jnp.arange(IMG_G, dtype=jnp.int32)
    owner = orders[:, group_member % N_PAIRS]
    depth = group_member // N_PAIRS
    span = IMG_DEV // CAP
    first = jax.random.randint(first_key, (N_PAIRS, IMG_G), 0, span)
    second = jax.random.randint(second_key, (N_PAIRS, IMG_G), 0, span)
    local_row = (jnp.minimum(first, second) + depth[None, :] * span) % IMG_DEV
    stored = owner * IMG_DEV + local_row
    return (image_slot, stored_image[stored].reshape(-1).astype(jnp.int32))


def draw_image_slot(key, part):
    return ownership_tables(key)[0]


def draw_group_images(key, part):
    return ownership_tables(key)[1]


def draw_picture_descriptors(key, part):
    base_key = jax.random.fold_in(jax.random.fold_in(key, 11), 0)
    base = jnp.clip(jax.random.normal(base_key, (IMAGES, TOKENS_IMG, DESCRIPTOR_DEPTH), jnp.float32), -6.0, 6.0) * 2.0
    values = base
    return values.astype(jnp.bfloat16)


def plant(entries, rng, smallest, high):
    shape = entries.shape
    place = [jax.random.randint(jax.random.fold_in(rng, axis), (), 0, shape[axis]) for axis in range(len(shape))]
    entries = entries.at[tuple(place)].set(smallest)
    longest = shape.index(max(shape))
    place[longest] = (place[longest] + 1) % shape[longest]
    return entries.at[tuple(place)].set(high)


def rank_bounds(number_of, slope):
    loads = [(1 << 20) // math.isqrt(standing ** slope) + 1 for standing in range(1, number_of + 1)]
    scale = 1 + sum(loads) // (1 << 30)
    return np.cumsum(np.array([max(1, weight // scale) for weight in loads]))


def skewed_ids(own_key, extent, amount, slope):
    listing = rank_bounds(amount, slope)
    lot = jax.random.randint(jax.random.fold_in(own_key, 1), extent, 0, int(listing[amount - 1]))
    rank = jnp.searchsorted(jnp.asarray(listing, jnp.int32), lot, side="right")
    return jax.random.permutation(jax.random.fold_in(own_key, 2), amount)[rank].astype(jnp.int32)


def length_profile(number_of, total, bound, lean):
    portions = [(1 << 20) // math.isqrt(rank ** lean) + 1 for rank in range(2, number_of + 1)]
    surplus, counts = total - bound - (number_of - 1), [1] * (number_of - 1)
    while surplus > 0:
        candidates = [i for i in range(number_of - 1) if counts[i] < bound]
        mass, budget = sum([portions[i] for i in candidates]), surplus
        for i in candidates:
            extra = min(bound - counts[i], max(1, budget * portions[i] // mass), surplus)
            counts[i] = counts[i] + extra
            surplus = surplus - extra
    return np.array([bound] + counts)


def ragged(own_key, amount, total, bound, slope):
    if amount == 2:
        one = jax.random.randint(own_key, (), max(1, total - bound), min(bound, total - 1) + 1)
        return jnp.stack([one, total - one])
    lengths = jnp.asarray(length_profile(amount, total, bound, slope), jnp.int32)
    couples = (amount - 1) // 2
    source_of, receiver = lengths[1:1 + 2 * couples:2], lengths[2:2 + 2 * couples:2]
    slack = jnp.minimum(source_of - 1, bound - receiver)
    moved = jax.random.randint(jax.random.fold_in(own_key, 1), (couples,), 0, 1 << 20) % (slack + 1)
    lengths = lengths.at[1:1 + 2 * couples:2].set(source_of - moved).at[2:2 + 2 * couples:2].set(receiver + moved)
    return lengths[jax.random.permutation(jax.random.fold_in(own_key, 2), amount)]


def setup_inputs(seed: int = 0) -> dict:
    key_of = jax.random.split(jax.random.key(seed), 6)
    picture_descriptors = draw_picture_descriptors(jax.random.fold_in(key_of[5], 71), 0)
    image_slot = draw_image_slot(jax.random.fold_in(key_of[5], 71), 0)
    group_images = draw_group_images(jax.random.fold_in(key_of[5], 71), 0)
    pair_target = plant(skewed_ids(key_of[3], (PAIRS,), TGT_G, 2), jax.random.fold_in(key_of[3], 3), 0, TGT_G - 1).astype(jnp.int32)
    pair_count = ragged(key_of[4], GROUPS, N_PAIRS * PAIR_G * 5 // 8, PAIR_G, 2).astype(jnp.int32)
    return dict(picture_descriptors=picture_descriptors, image_slot=image_slot, group_images=group_images, pair_target=pair_target, pair_count=pair_count)


SHARPNESS_DIVISOR = 0.1


def reference(picture_descriptors, image_slot, group_images, pair_target, pair_count):
    token = jnp.arange(TOKENS_IMG, dtype=jnp.int32)
    horizontal_grid = (2.0 * (token % IMG_W).astype(jnp.float32) + 1.0) / IMG_W - 1.0
    coord_y = (2.0 * (token // IMG_W).astype(jnp.float32) + 1.0) / IMG_H - 1.0
    similarity_multiplier = 1.0 / (DESCRIPTOR_DEPTH * SHARPNESS_DIVISOR)

    def one_pair(index):
        group = index // PAIR_G
        within_group = index % PAIR_G
        query_id = group_images[group * IMG_G + TGT_G + within_group]
        target_id = group_images[group * IMG_G + pair_target[index]]
        query = picture_descriptors[image_slot[query_id]]
        target = picture_descriptors[image_slot[target_id]]
        match_scores = jnp.dot(query, target.T, preferred_element_type=jnp.float32) * similarity_multiplier
        row_exp = jnp.exp(match_scores - jnp.max(match_scores, axis=1, keepdims=True))
        row_prob = row_exp / jnp.sum(row_exp, axis=1, keepdims=True)
        col_exp = jnp.exp(match_scores - jnp.max(match_scores, axis=0, keepdims=True))
        col_prob = col_exp / jnp.sum(col_exp, axis=0, keepdims=True)
        field = jnp.stack([jnp.sum(row_prob * horizontal_grid[None, :], axis=1),
                           jnp.sum(row_prob * coord_y[None, :], axis=1),
                           jnp.sum(row_prob * col_prob, axis=1)])
        valid = (within_group < pair_count[group]).astype(jnp.float32)
        return field * valid

    return lax.map(one_pair, jnp.arange(PAIRS, dtype=jnp.int32))
```

```python
import functools
import math

import jax
import jax.numpy as jnp
from jax import lax
from jax.experimental import pallas as pl
from jax.experimental.pallas import tpu as pltpu
from jax.sharding import PartitionSpec as P

IMG_W = 64
TGT_G = 8
SHARPNESS_DIVISOR = 0.1
LOG2E = math.log2(math.e)
LANES = 128
CAPACITIES = (4, 5, 6, 7, 8, 10)


def match_kernel(image_rows, multiplier, meta, q0, q1, q2, q3, target, out, scores, column):
    quad = meta[0]
    slab = target.shape[1]
    queries = (q0, q1, q2, q3)
    quads = len(queries)

    @pl.when(pl.program_id(0) < meta[1])
    def _():
        for step, query in enumerate(queries):
            scores[:, step * slab : (step + 1) * slab] = (
                lax.dot_general(
                    target[0], query[0], (((1,), (1,)), ((), ())), preferred_element_type=jnp.float32
                )
                * multiplier
            )

        def rows_step(index, carry):
            rows = pl.ds(pl.multiple_of(index * 16, 16), 16)
            block = scores[rows, :]
            top = jnp.max(block, axis=1, keepdims=True)
            powers = jnp.exp2(block - top)
            column[rows, :] = powers * (1.0 / jnp.sum(powers, axis=1, keepdims=True))
            return carry

        lax.fori_loop(0, slab // 16, rows_step, 0, unroll=2)

        bands = slab // IMG_W
        along = lax.broadcasted_iota(jnp.int32, (IMG_W, LANES), 0).astype(jnp.float32)
        coord_x = (2.0 * along + 1.0) / IMG_W - 1.0
        first_row = quad * bands
        for step in range(quads):
            slot = lax.rem(quad - step + quads, quads)

            def lanes_step(index, carry, step=step, slot=slot):
                lanes = pl.ds(pl.multiple_of(step * slab + index * LANES, LANES), LANES)
                block = scores[:, lanes]
                top = jnp.max(block, axis=0, keepdims=True)
                total = jnp.zeros((8, LANES), jnp.float32)
                weighted_y = jnp.zeros((8, LANES), jnp.float32)
                mutual = jnp.zeros((8, LANES), jnp.float32)
                folded = jnp.zeros((IMG_W, LANES), jnp.float32)
                for band in range(bands):
                    piece = slice(band * IMG_W, (band + 1) * IMG_W)
                    powers = jnp.exp2(block[piece] - top)
                    folded += powers
                    part = jnp.sum(powers.reshape(IMG_W // 8, 8, LANES), axis=0)
                    total += part
                    coord_y = (2.0 * (first_row + band).astype(jnp.float32) + 1.0) / image_rows - 1.0
                    weighted_y += part * coord_y
                    mutual += jnp.sum((powers * column[piece, lanes]).reshape(IMG_W // 8, 8, LANES), axis=0)
                place = pl.ds(pl.multiple_of(index * LANES, LANES), LANES)
                out[slot, 0, 0:1, place] = top
                out[slot, 0, 1:2, place] = jnp.sum(total, axis=0, keepdims=True)
                out[slot, 0, 2:3, place] = jnp.sum(folded * coord_x, axis=0, keepdims=True)
                out[slot, 0, 3:4, place] = jnp.sum(weighted_y, axis=0, keepdims=True)
                out[slot, 0, 4:5, place] = jnp.sum(mutual, axis=0, keepdims=True)
                return carry

            lax.fori_loop(0, slab // LANES, lanes_step, 0)


def match(image_rows, multiplier, meta, queries, target):
    pairs, slab, width = target.shape
    quads = len(queries)
    block = pl.BlockSpec((1, slab, width), lambda pair, meta: (pair, 0, 0))
    return pl.pallas_call(
        functools.partial(match_kernel, image_rows, multiplier),
        grid_spec=pltpu.PrefetchScalarGridSpec(
            num_scalar_prefetch=1,
            grid=(pairs,),
            in_specs=[block] * (quads + 1),
            out_specs=pl.BlockSpec((quads, 1, 8, slab), lambda pair, meta: (0, pair, 0, 0)),
            scratch_shapes=[pltpu.VMEM((slab, quads * slab), jnp.float32)] * 2,
        ),
        out_shape=jax.ShapeDtypeStruct((quads, pairs, 8, slab), jnp.float32),
        compiler_params=pltpu.CompilerParams(vmem_limit_bytes=40 * 1024 * 1024),
        cost_estimate=pl.CostEstimate(
            flops=2 * pairs * slab * slab * quads * width, bytes_accessed=4 << 20, transcendentals=4 << 20
        ),
    )(meta, *queries, target)


def shards(picture_descriptors, image_slot, group_images, pair_target, pair_count):
    groups = lax.axis_size("pairs")
    quads = lax.axis_size("quad")
    me = lax.axis_index("pairs")
    quad = lax.axis_index("quad")
    images_dev, slab, width = picture_descriptors.shape
    pairs = pair_target.shape[0]
    images = image_slot.shape[0]
    piece = slab // groups
    image_rows = slab * quads // IMG_W
    multiplier = LOG2E / (width * SHARPNESS_DIVISOR)

    position = jnp.arange(group_images.shape[0], dtype=jnp.int32)
    wanted = jnp.concatenate([TGT_G + jnp.arange(pairs, dtype=jnp.int32), pair_target])
    ids = jnp.sum(jnp.where(wanted[:, None] == position[None, :], group_images[None, :], 0), axis=1)
    catalog = jnp.arange(images, dtype=jnp.int32)
    stored = jnp.sum(jnp.where(ids[:, None] == catalog[None, :], image_slot[None, :], 0), axis=1)
    in_use = jnp.arange(pairs, dtype=jnp.int32) < pair_count[0]
    stored = jnp.where(jnp.concatenate([in_use, in_use]), stored, -1)
    asked = lax.all_to_all(
        jnp.broadcast_to(stored[None, :], (groups, 2 * pairs)), "pairs", split_axis=0, concat_axis=0, tiled=True
    )

    flat = asked.reshape(-1)
    asked_row = jnp.any(flat[:, None] == catalog[None, :], axis=0)
    per_owner = asked_row.reshape(groups, images_dev).astype(jnp.int32)
    most = jnp.max(jnp.sum(per_owner, axis=1))
    before = (flat[:, None] > catalog[None, :]) & (flat[:, None] // images_dev == catalog[None, :] // images_dev)
    place = jnp.sum((before & asked_row[None, :]).astype(jnp.int32), axis=1)
    owner = jnp.maximum(flat, 0) // images_dev
    mine = lax.dynamic_index_in_dim(per_owner, me, 0, keepdims=False)
    row = jnp.arange(images_dev, dtype=jnp.int32)
    my_place = jnp.sum(jnp.where(row[:, None] > row[None, :], mine[None, :], 0), axis=1)

    def exchange(capacity, operands):
        descriptors, mine, my_place, owner, place = operands
        slots = jnp.arange(capacity, dtype=jnp.int32)
        rows = jnp.sum(
            jnp.where((my_place[None, :] == slots[:, None]) & (mine[None, :] > 0), row[None, :], 0), axis=1
        )
        picked = jnp.take(descriptors, rows, axis=0)
        pieces = picked.reshape(capacity, groups, piece, width).transpose(1, 0, 2, 3)
        spread = lax.all_to_all(pieces, "pairs", split_axis=0, concat_axis=0, tiled=True)
        spread = spread.reshape(groups * capacity, piece, width)
        index = (owner * capacity + jnp.minimum(place, capacity - 1)).reshape(groups, 2, pairs)
        return tuple(
            jnp.take(spread, index[:, part].reshape(-1), axis=0).reshape(groups, pairs, piece, width)
            for part in range(2)
        )

    capacities = [size for size in CAPACITIES if size < images_dev] + [images_dev]
    branch = jnp.sum(jnp.asarray(capacities, jnp.int32) < most)
    for_query, for_target = lax.switch(
        branch,
        [functools.partial(exchange, size) for size in capacities],
        (picture_descriptors, mine, my_place, owner, place),
    )

    def deliver(pieces):
        arrived = lax.all_to_all(pieces, "pairs", split_axis=0, concat_axis=0, tiled=True)
        return arrived.transpose(1, 0, 2, 3).reshape(pairs, slab, width)

    query = deliver(for_query)
    target = deliver(for_target)
    queries = [query] + [
        lax.ppermute(query, "quad", [(i, (i + step) % quads) for i in range(quads)]) for step in range(1, quads)
    ]
    meta = jnp.stack([quad.astype(jnp.int32), pair_count[0]])
    partial = match(image_rows, multiplier, meta, queries, target)
    partial = lax.all_to_all(partial, "quad", split_axis=0, concat_axis=0, tiled=True)
    top = partial[:, :, 0:1]
    weight = jnp.exp2(top - jnp.max(top, axis=0, keepdims=True))
    sums = jnp.sum(partial[:, :, 1:5] * weight, axis=0)
    return jnp.where(in_use[:, None, None], sums[:, 1:4] / sums[:, 0:1], 0.0)


def solution(mesh):
    return jax.shard_map(
        shards,
        mesh=mesh,
        in_specs=(P("pairs", "quad", None), P(), P("pairs"), P("pairs"), P("pairs")),
        out_specs=P("pairs", None, "quad"),
        check_vma=False,
    )
```

```python
import functools
import math

import jax
import jax.numpy as jnp
from jax import lax
from jax.experimental import pallas as pl
from jax.experimental.pallas import tpu as pltpu
from jax.sharding import PartitionSpec as P

IMG_W = 64
TGT_G = 8
SHARPNESS_DIVISOR = 0.1
LOG2E = math.log2(math.e)
LANES = 128
CORES = 2
PLACES = 64
CAPACITIES = (6, 7, 8, 9, 10, 11, 12, 16)
ANY = pl.BlockSpec(memory_space=pl.ANY)
SMEM = pl.BlockSpec(memory_space=pltpu.SMEM)
VMEM = pl.BlockSpec(memory_space=pltpu.VMEM)


def plan_kernel(chip_rows, entries, chip, asked, index, rows, most, requested, before):
    groups = asked.shape[0]
    tiles = requested.shape[0]
    table = asked[:, 0, :]
    lane = lax.broadcasted_iota(jnp.int32, (groups, LANES), 1)
    columns = [table[:, entry : entry + 1] for entry in range(entries)]
    for tile in range(tiles):
        hit = columns[0] == lane + tile * LANES
        for column in columns[1:]:
            hit = hit | (column == lane + tile * LANES)
        requested[tile : tile + 1, :] = jnp.max(jnp.where(hit, 1.0, 0.0), axis=0, keepdims=True)
    first = lax.broadcasted_iota(jnp.int32, (LANES, LANES), 0)
    second = lax.broadcasted_iota(jnp.int32, (LANES, LANES), 1)
    earlier = (first < second) & (lax.div(first, chip_rows) == lax.div(second, chip_rows))
    flags = requested[...]
    before[...] = jnp.dot(flags, jnp.where(earlier, 1.0, 0.0), preferred_element_type=jnp.float32)
    most[0] = jnp.max(before[...] + flags).astype(jnp.int32)

    codes = jnp.zeros((groups, LANES), jnp.int32)
    for entry, column in enumerate(columns):
        found = jnp.zeros((groups, LANES), jnp.float32)
        for tile in range(tiles):
            found += jnp.where(column == lane + tile * LANES, before[tile : tile + 1, :], 0.0)
        place = jnp.sum(found, axis=1, keepdims=True).astype(jnp.int32)
        code = lax.div(jnp.maximum(column, 0), chip_rows) * PLACES + place
        codes = jnp.where(lane == entry, code, codes)
    index[...] = codes

    chips_tile = LANES // chip_rows
    tile = lax.div(chip[0], chips_tile)
    part = lax.rem(chip[0], chips_tile)
    slot = lax.broadcasted_iota(jnp.int32, (chip_rows, LANES), 0).astype(jnp.float32)
    along = lax.broadcasted_iota(jnp.int32, (chip_rows, LANES), 1)
    mine = (requested[pl.ds(tile, 1), :] > 0.0) & (before[pl.ds(tile, 1), :] == slot)
    mine = mine & (lax.div(along, chip_rows) == part)
    row = jnp.sum(jnp.where(mine, lax.rem(along, chip_rows), 0).astype(jnp.float32), axis=1, keepdims=True)
    rows[...] = jnp.broadcast_to(row.astype(jnp.int32), rows.shape)


def plan(chip_rows, images, entries, chip, asked):
    groups = asked.shape[0]
    return pl.pallas_call(
        functools.partial(plan_kernel, chip_rows, entries),
        in_specs=[SMEM, VMEM],
        out_specs=(VMEM, VMEM, SMEM),
        out_shape=(
            jax.ShapeDtypeStruct((groups, LANES), jnp.int32),
            jax.ShapeDtypeStruct((chip_rows, LANES), jnp.int32),
            jax.ShapeDtypeStruct((1,), jnp.int32),
        ),
        scratch_shapes=[pltpu.VMEM((images // LANES, LANES), jnp.float32)] * 2,
    )(chip, asked)


def pick_kernel(core, rows, own, other, out, sems):
    images_dev = own.shape[0]
    half = other.shape[-1]
    capacity = out.shape[1]
    features = pl.ds(pl.multiple_of(core[0] * half, LANES), half)
    for slot in range(capacity):
        row = rows[slot, 0]
        local = lax.rem(row, images_dev)
        is_own = lax.div(row, images_dev) == core[0]

        @pl.when(is_own)
        def _():
            pltpu.make_async_copy(own.at[local, :, :, features], out.at[:, slot], sems.at[slot]).start()

        @pl.when(jnp.logical_not(is_own))
        def _():
            pltpu.make_async_copy(other.at[local], out.at[:, slot], sems.at[slot]).start()

    for slot in range(capacity):
        pltpu.make_async_copy(other.at[0], out.at[:, slot], sems.at[slot]).wait()


def pick(capacity, core, rows, own, other):
    images_dev, groups, piece, half = other.shape
    return pl.pallas_call(
        pick_kernel,
        in_specs=[SMEM, SMEM, ANY, ANY],
        out_specs=ANY,
        out_shape=jax.ShapeDtypeStruct((groups, capacity, piece, half), other.dtype),
        scratch_shapes=[pltpu.SemaphoreType.DMA((capacity,))],
    )(core, rows, own, other)


def regroup_kernel(index, spread, for_query, for_target):
    groups, pairs = for_query.shape[:2]
    half = spread.shape[-1]

    def step(group, carry):
        for entry in range(2 * pairs):
            code = index[group, entry]
            chip = lax.div(code, PLACES)
            place = lax.rem(code, PLACES)
            target = for_query if entry < pairs else for_target
            for core in range(CORES):
                target[group, entry % pairs, :, core * half : (core + 1) * half] = spread[chip * CORES + core, place]
        return carry

    lax.fori_loop(0, groups, step, 0, unroll=4)


def regroup(pairs, index, spread):
    groups, _, piece, half = spread.shape
    shape = jax.ShapeDtypeStruct((groups, pairs, piece, CORES * half), spread.dtype)
    return pl.pallas_call(
        regroup_kernel,
        in_specs=[SMEM, VMEM],
        out_specs=(VMEM, VMEM),
        out_shape=(shape, shape),
        compiler_params=pltpu.CompilerParams(vmem_limit_bytes=24 * 1024 * 1024),
    )(index, spread)


def match_kernel(image_rows, multiplier, meta, q0, q1, q2a, q2b, q3, target, out, scores, column):
    quad = meta[0]
    width = target.shape[-1]
    slab = target.shape[0] * target.shape[2]
    quads = out.shape[0]

    @pl.when(pl.program_id(0) < meta[1])
    def _():
        rows = target[:, 0].reshape(slab, width)
        start = 0
        for query in (q0, q1, q2a, q2b, q3):
            tokens = query.shape[0] * query.shape[2]
            scores[:, start : start + tokens] = (
                lax.dot_general(
                    rows, query[:, 0].reshape(tokens, width), (((1,), (1,)), ((), ())),
                    preferred_element_type=jnp.float32,
                )
                * multiplier
            )
            start += tokens

        def rows_step(index, carry):
            block = pl.ds(pl.multiple_of(index * 32, 32), 32)
            top = jnp.max(scores[block, :], axis=1, keepdims=True)
            powers = jnp.exp2(scores[block, :] - top)
            column[block, :] = powers * (1.0 / jnp.sum(powers, axis=1, keepdims=True))
            return carry

        lax.fori_loop(0, slab // 32, rows_step, 0, unroll=4)

        bands = slab // IMG_W
        along = lax.broadcasted_iota(jnp.int32, (IMG_W, LANES), 0).astype(jnp.float32)
        coord_x = (2.0 * along + 1.0) / IMG_W - 1.0
        first_row = quad * bands
        for step in range(quads):
            slot = lax.rem(quad - step + quads, quads)

            def lanes_step(index, carry, step=step, slot=slot):
                lanes = pl.ds(pl.multiple_of(step * slab + index * LANES, LANES), LANES)
                top = jnp.max(scores[:, lanes], axis=0, keepdims=True)
                total = jnp.zeros((8, LANES), jnp.float32)
                weighted_y = jnp.zeros((8, LANES), jnp.float32)
                mutual = jnp.zeros((8, LANES), jnp.float32)
                folded = jnp.zeros((IMG_W, LANES), jnp.float32)
                for band in range(bands):
                    piece = slice(band * IMG_W, (band + 1) * IMG_W)
                    powers = jnp.exp2(scores[piece, lanes] - top)
                    folded += powers
                    part = jnp.sum(powers.reshape(IMG_W // 8, 8, LANES), axis=0)
                    total += part
                    coord_y = (2.0 * (first_row + band).astype(jnp.float32) + 1.0) / image_rows - 1.0
                    weighted_y += part * coord_y
                    mutual += jnp.sum((powers * column[piece, lanes]).reshape(IMG_W // 8, 8, LANES), axis=0)
                place = pl.ds(pl.multiple_of(index * LANES, LANES), LANES)
                out[slot, 0, 0:1, place] = top
                out[slot, 0, 1:2, place] = jnp.sum(total, axis=0, keepdims=True)
                out[slot, 0, 2:3, place] = jnp.sum(folded * coord_x, axis=0, keepdims=True)
                out[slot, 0, 3:4, place] = jnp.sum(weighted_y, axis=0, keepdims=True)
                out[slot, 0, 4:5, place] = jnp.sum(mutual, axis=0, keepdims=True)
                return carry

            lax.fori_loop(0, slab // LANES, lanes_step, 0, unroll=4)


def match(image_rows, multiplier, meta, quads, queries, target):
    pieces, pairs, piece, width = target.shape
    slab = pieces * piece

    def block(array):
        return pl.BlockSpec((array.shape[0], 1, piece, width), lambda pair, meta: (0, pair, 0, 0))

    return pl.pallas_call(
        functools.partial(match_kernel, image_rows, multiplier),
        grid_spec=pltpu.PrefetchScalarGridSpec(
            num_scalar_prefetch=1,
            grid=(pairs,),
            in_specs=[block(array) for array in (*queries, target)],
            out_specs=pl.BlockSpec((quads, 1, 8, slab), lambda pair, meta: (0, pair, 0, 0)),
            scratch_shapes=[pltpu.VMEM((slab, quads * slab), jnp.float32)] * 2,
        ),
        out_shape=jax.ShapeDtypeStruct((quads, pairs, 8, slab), jnp.float32),
        compiler_params=pltpu.CompilerParams(vmem_limit_bytes=40 * 1024 * 1024),
        cost_estimate=pl.CostEstimate(
            flops=2 * pairs * slab * slab * quads * width, bytes_accessed=4 << 20, transcendentals=4 << 20
        ),
    )(meta, *queries, target)


def shards(picture_descriptors, image_slot, group_images, pair_target, pair_count):
    groups = lax.axis_size("pairs")
    quads = lax.axis_size("quad")
    me = lax.axis_index("pairs").astype(jnp.int32)
    quad = lax.axis_index("quad").astype(jnp.int32)
    images_dev, slab, width = picture_descriptors.shape
    pairs = pair_target.shape[0]
    images = image_slot.shape[0]
    piece = slab // groups
    half = width // CORES
    chip_rows = images_dev * CORES
    image_rows = slab * quads // IMG_W
    multiplier = LOG2E / (width * SHARPNESS_DIVISOR)
    core = me % CORES

    position = jnp.arange(group_images.shape[0], dtype=jnp.int32)
    wanted = jnp.concatenate([TGT_G + jnp.arange(pairs, dtype=jnp.int32), pair_target])
    ids = jnp.sum(jnp.where(wanted[:, None] == position[None, :], group_images[None, :], 0), axis=1)
    catalog = jnp.arange(images, dtype=jnp.int32)
    stored = jnp.sum(jnp.where(ids[:, None] == catalog[None, :], image_slot[None, :], 0), axis=1)
    in_use = jnp.arange(pairs, dtype=jnp.int32) < pair_count[0]
    stored = jnp.where(jnp.concatenate([in_use, in_use]), stored, -1)
    message = jnp.pad(stored, (0, LANES - 2 * pairs), constant_values=-1)
    asked = lax.all_to_all(
        jnp.broadcast_to(message[None, None, :], (groups, 1, LANES)), "pairs", split_axis=0, concat_axis=0, tiled=True
    )

    given = lax.dynamic_slice_in_dim(picture_descriptors, (CORES - 1 - core) * half, half, axis=2)
    traded = lax.ppermute(given, "pairs", [(i, i ^ 1) for i in range(groups)])

    index, rows, most = plan(chip_rows, images, 2 * pairs, (me // CORES)[None], asked)
    own = picture_descriptors.reshape(images_dev, groups, piece, width)
    other = traded.reshape(images_dev, groups, piece, half)

    def exchange(capacity, operands):
        own, other, rows, index = operands
        pieces = pick(capacity, core[None], rows, own, other)
        spread = lax.all_to_all(pieces, "pairs", split_axis=0, concat_axis=0, tiled=True)
        return regroup(pairs, index, spread)

    capacities = [size for size in CAPACITIES if size < chip_rows] + [chip_rows]
    branch = jnp.sum(jnp.asarray(capacities, jnp.int32) < most[0])
    for_query, for_target = lax.switch(
        branch, [functools.partial(exchange, size) for size in capacities], (own, other, rows, index)
    )

    def move(array, step):
        return lax.ppermute(array, "quad", [(i, (i + step) % quads) for i in range(quads)])

    query = lax.all_to_all(for_query, "pairs", split_axis=0, concat_axis=0, tiled=True)
    before = move(query, 1)
    after = move(query, quads - 1)
    across = (move(before[: groups // 2], 1), move(after[groups // 2 :], quads - 1))
    target = lax.all_to_all(for_target, "pairs", split_axis=0, concat_axis=0, tiled=True)
    meta = jnp.stack([quad, pair_count[0]])
    partial = match(image_rows, multiplier, meta, quads, (query, before, *across, after), target)
    partial = lax.all_to_all(partial, "quad", split_axis=0, concat_axis=0, tiled=True)
    top = partial[:, :, 0:1]
    weight = jnp.exp2(top - jnp.max(top, axis=0, keepdims=True))
    sums = jnp.sum(partial[:, :, 1:5] * weight, axis=0)
    return jnp.where(in_use[:, None, None], sums[:, 1:4] / sums[:, 0:1], 0.0)


def solution(mesh):
    return jax.shard_map(
        shards,
        mesh=mesh,
        in_specs=(P("pairs", "quad", None), P(), P("pairs"), P("pairs"), P("pairs")),
        out_specs=P("pairs", None, "quad"),
        check_vma=False,
    )
```

```python
import functools
import math

import jax
import jax.numpy as jnp
from jax import lax
from jax.experimental import pallas as pl
from jax.experimental.pallas import tpu as pltpu
from jax.sharding import Mesh
from jax.sharding import PartitionSpec as P

IMG_W = 64
TGT_G = 8
SHARPNESS_DIVISOR = 0.1
LOG2E = math.log2(math.e)
LANES = 128
CORES = 2
PLACES = 64
CAPACITIES = (6, 7, 8, 9, 10, 11, 12, 16)
ANY = pl.BlockSpec(memory_space=pl.ANY)
SMEM = pl.BlockSpec(memory_space=pltpu.SMEM)
VMEM = pl.BlockSpec(memory_space=pltpu.VMEM)


def plan_kernel(chip_rows, entries, capacities, chip, asked, index, rows, branch, requested, before):
    groups = asked.shape[0]
    table = asked[:, 0, :]
    lane = lax.broadcasted_iota(jnp.int32, (groups, LANES), 1)
    chips, locals_ = [], []
    count = jnp.zeros((LANES, LANES), jnp.float32)
    for entry in range(entries):
        stored = table[:, entry : entry + 1]
        chips.append(jnp.where(lax.div(stored, chip_rows) == lane, 1.0, 0.0) * jnp.where(stored >= 0, 1.0, 0.0))
        locals_.append(jnp.where(lax.rem(stored, chip_rows) == lane, 1.0, 0.0))
        count += lax.dot_general(
            chips[-1], locals_[-1], (((0,), (0,)), ((), ())), preferred_element_type=jnp.float32
        )
    flags = jnp.where(count > 0.0, 1.0, 0.0)
    first = lax.broadcasted_iota(jnp.int32, (LANES, LANES), 0)
    second = lax.broadcasted_iota(jnp.int32, (LANES, LANES), 1)
    earlier = jnp.dot(flags, jnp.where(first < second, 1.0, 0.0), preferred_element_type=jnp.float32)
    requested[...] = flags
    before[...] = earlier
    most = jnp.max(earlier + flags)
    choice = jnp.int32(0)
    for capacity in capacities[:-1]:
        choice += jnp.where(most > capacity, 1, 0)
    branch[0] = choice

    codes = jnp.zeros((groups, LANES), jnp.int32)
    for entry in range(entries):
        places = jnp.dot(chips[entry], earlier, preferred_element_type=jnp.float32) * locals_[entry]
        place = jnp.sum(places, axis=1, keepdims=True).astype(jnp.int32)
        stored = jnp.maximum(table[:, entry : entry + 1], 0)
        codes = jnp.where(lane == entry, lax.div(stored, chip_rows) * PLACES + place, codes)
    index[...] = codes

    mine = chip[0]
    slot = lax.broadcasted_iota(jnp.int32, (chip_rows, LANES), 0).astype(jnp.float32)
    along = lax.broadcasted_iota(jnp.int32, (chip_rows, LANES), 1).astype(jnp.float32)
    chosen = (requested[pl.ds(mine, 1), :] > 0.0) & (before[pl.ds(mine, 1), :] == slot)
    row = jnp.sum(jnp.where(chosen, along, 0.0), axis=1, keepdims=True)
    rows[...] = jnp.broadcast_to(row.astype(jnp.int32), rows.shape)


def plan(chip_rows, entries, capacities, chip, asked):
    groups = asked.shape[0]
    return pl.pallas_call(
        functools.partial(plan_kernel, chip_rows, entries, capacities),
        grid=(1,),
        in_specs=[SMEM, pl.BlockSpec(asked.shape, lambda step: (0, 0, 0))],
        out_specs=(
            pl.BlockSpec((groups, LANES), lambda step: (0, 0)),
            pl.BlockSpec((chip_rows, LANES), lambda step: (0, 0)),
            SMEM,
        ),
        out_shape=(
            jax.ShapeDtypeStruct((groups, LANES), jnp.int32),
            jax.ShapeDtypeStruct((chip_rows, LANES), jnp.int32),
            jax.ShapeDtypeStruct((1,), jnp.int32),
        ),
        scratch_shapes=[pltpu.VMEM((LANES, LANES), jnp.float32)] * 2,
    )(chip, asked)


def pick_kernel(core, rows, own, other, out, sems):
    images_dev = own.shape[0]
    capacity = out.shape[1]
    for slot in range(capacity):
        row = rows[slot, 0]
        local = lax.rem(row, images_dev)
        is_own = lax.div(row, images_dev) == core[0]

        @pl.when(is_own)
        def _():
            pltpu.make_async_copy(own.at[local, core[0]], out.at[:, slot], sems.at[slot]).start()

        @pl.when(jnp.logical_not(is_own))
        def _():
            pltpu.make_async_copy(other.at[local, core[0]], out.at[:, slot], sems.at[slot]).start()

    for slot in range(capacity):
        pltpu.make_async_copy(other.at[0, 0], out.at[:, slot], sems.at[slot]).wait()


def pick(capacity, core, rows, own, other):
    _, _, chips, piece, width = other.shape
    return pl.pallas_call(
        pick_kernel,
        in_specs=[SMEM, SMEM, ANY, ANY],
        out_specs=VMEM,
        out_shape=jax.ShapeDtypeStruct((chips, capacity, piece, width), other.dtype),
        scratch_shapes=[pltpu.SemaphoreType.DMA((capacity,))],
        compiler_params=pltpu.CompilerParams(vmem_limit_bytes=24 * 1024 * 1024),
    )(core, rows, own, other)


def regroup_kernel(index, spread, out):
    groups, entries = out.shape[:2]

    def step(group, carry):
        for entry in range(entries):
            code = index[group, entry]
            out[group, entry] = spread[lax.div(code, PLACES), lax.rem(code, PLACES)]
        return carry

    lax.fori_loop(0, groups, step, 0, unroll=8)


def regroup(groups, entries, index, spread):
    return pl.pallas_call(
        regroup_kernel,
        in_specs=[SMEM, VMEM],
        out_specs=VMEM,
        out_shape=jax.ShapeDtypeStruct((groups, entries, *spread.shape[2:]), spread.dtype),
        compiler_params=pltpu.CompilerParams(vmem_limit_bytes=24 * 1024 * 1024),
    )(index, spread)


def match_kernel(image_rows, multiplier, pair, meta, q0, q1, q2a, q2b, q3, target, earlier, out, scores, column):
    quad = meta[0]
    chips, cores, _, piece, width = target.shape
    part = chips * piece
    slab = cores * part
    quads = out.shape[0]
    for previous in range(pair):
        out[:, previous] = earlier[:, previous]

    @pl.when(pair < meta[1])
    def _():
        for row in range(cores):
            rows = target[:, row, 0].reshape(part, width)
            for step, skip, query in ((0, 0, q0), (1, 0, q1), (2, 0, q2a), (2, q2a.shape[0], q2b), (3, 0, q3)):
                tokens = query.shape[0] * piece
                for core in range(cores):
                    start = step * slab + core * part + skip * piece
                    scores[row * part : (row + 1) * part, start : start + tokens] = (
                        lax.dot_general(
                            rows, query[:, core, 0].reshape(tokens, width), (((1,), (1,)), ((), ())),
                            preferred_element_type=jnp.float32,
                        )
                        * multiplier
                    )

        def rows_step(index, carry):
            block = pl.ds(pl.multiple_of(index * 32, 32), 32)
            top = jnp.max(scores[block, :], axis=1, keepdims=True)
            powers = jnp.exp2(scores[block, :] - top)
            column[block, :] = powers * (1.0 / jnp.sum(powers, axis=1, keepdims=True))
            return carry

        lax.fori_loop(0, slab // 32, rows_step, 0, unroll=4)

        bands = slab // IMG_W
        along = lax.broadcasted_iota(jnp.int32, (IMG_W, LANES), 0).astype(jnp.float32)
        coord_x = (2.0 * along + 1.0) / IMG_W - 1.0
        first_row = quad * bands
        for step in range(quads):
            slot = lax.rem(quad - step + quads, quads)

            def lanes_step(index, carry, step=step, slot=slot):
                lanes = pl.ds(pl.multiple_of(step * slab + index * LANES, LANES), LANES)
                top = jnp.max(scores[:, lanes], axis=0, keepdims=True)
                total = jnp.zeros((8, LANES), jnp.float32)
                weighted_y = jnp.zeros((8, LANES), jnp.float32)
                mutual = jnp.zeros((8, LANES), jnp.float32)
                folded = jnp.zeros((IMG_W, LANES), jnp.float32)
                for band in range(bands):
                    piece = slice(band * IMG_W, (band + 1) * IMG_W)
                    powers = jnp.exp2(scores[piece, lanes] - top)
                    folded += powers
                    part = jnp.sum(powers.reshape(IMG_W // 8, 8, LANES), axis=0)
                    total += part
                    coord_y = (2.0 * (first_row + band).astype(jnp.float32) + 1.0) / image_rows - 1.0
                    weighted_y += part * coord_y
                    mutual += jnp.sum((powers * column[piece, lanes]).reshape(IMG_W // 8, 8, LANES), axis=0)
                place = pl.ds(pl.multiple_of(index * LANES, LANES), LANES)
                out[slot, pair, 0:1, place] = top
                out[slot, pair, 1:2, place] = jnp.sum(total, axis=0, keepdims=True)
                out[slot, pair, 2:3, place] = jnp.sum(folded * coord_x, axis=0, keepdims=True)
                out[slot, pair, 3:4, place] = jnp.sum(weighted_y, axis=0, keepdims=True)
                out[slot, pair, 4:5, place] = jnp.sum(mutual, axis=0, keepdims=True)
                return carry

            lax.fori_loop(0, slab // LANES, lanes_step, 0, unroll=4)


def match(image_rows, multiplier, pair, meta, queries, maps, earlier):
    chips, cores, entries, piece, width = maps.shape
    quads = len(queries)
    pairs = entries // 2
    slab = chips * cores * piece

    def block(array, entry=0):
        return pl.BlockSpec((array.shape[0], cores, 1, piece, width), lambda step, meta: (0, 0, entry, 0, 0))

    partials = (quads, pairs, 8, slab)
    done = pl.BlockSpec((quads, max(pair, 1), 8, slab), lambda step, meta: (0, 0, 0, 0))
    return pl.pallas_call(
        functools.partial(match_kernel, image_rows, multiplier, pair),
        grid_spec=pltpu.PrefetchScalarGridSpec(
            num_scalar_prefetch=1,
            grid=(1,),
            in_specs=[block(maps, pair)] + [block(array) for array in queries] + [block(maps, pairs + pair), done],
            out_specs=pl.BlockSpec((quads, pair + 1, 8, slab), lambda step, meta: (0, 0, 0, 0)),
            scratch_shapes=[pltpu.VMEM((slab, quads * slab), jnp.float32)] * 2,
        ),
        out_shape=jax.ShapeDtypeStruct((quads, pair + 1, 8, slab), jnp.float32),
        compiler_params=pltpu.CompilerParams(vmem_limit_bytes=40 * 1024 * 1024),
        cost_estimate=pl.CostEstimate(
            flops=2 * slab * slab * quads * width, bytes_accessed=2 << 20, transcendentals=2 << 20
        ),
    )(meta, maps, *queries, maps, earlier)


def shards(picture_descriptors, image_slot, group_images, pair_target, pair_count):
    chips = lax.axis_size("chip")
    cores = lax.axis_size("core")
    quads = lax.axis_size("quad")
    groups = chips * cores
    chip = lax.axis_index("chip").astype(jnp.int32)
    core = lax.axis_index("core").astype(jnp.int32)
    quad = lax.axis_index("quad").astype(jnp.int32)
    images_dev, slab, width = picture_descriptors.shape
    pairs = pair_target.shape[0]
    images = image_slot.shape[0]
    chip_rows = images_dev * cores
    image_rows = slab * quads // IMG_W
    multiplier = LOG2E / (width * SHARPNESS_DIVISOR)

    def all_pairs(array):
        return lax.all_to_all(array, ("chip", "core"), split_axis=0, concat_axis=0, tiled=True)

    traded = lax.ppermute(picture_descriptors, "core", [(i, (i + 1) % cores) for i in range(cores)])

    position = jnp.arange(group_images.shape[0], dtype=jnp.int32)
    wanted = jnp.concatenate([TGT_G + jnp.arange(pairs, dtype=jnp.int32), pair_target])
    ids = jnp.sum(jnp.where(wanted[:, None] == position[None, :], group_images[None, :], 0), axis=1)
    catalog = jnp.arange(images, dtype=jnp.int32)
    stored = jnp.sum(jnp.where(ids[:, None] == catalog[None, :], image_slot[None, :], 0), axis=1)
    in_use = jnp.arange(pairs, dtype=jnp.int32) < pair_count[0]
    stored = jnp.where(jnp.concatenate([in_use, in_use]), stored, -1)
    message = jnp.pad(stored, (0, LANES - 2 * pairs), constant_values=-1)
    asked = all_pairs(jnp.broadcast_to(message[None, None, :], (groups, 1, LANES)))

    capacities = [size for size in CAPACITIES if size < chip_rows] + [chip_rows]
    index, rows, branch = plan(chip_rows, 2 * pairs, capacities, chip[None], asked)
    halves = (images_dev, cores, chips, slab // groups, width)

    def exchange(capacity, operands):
        own, other, rows, index = operands
        pieces = pick(capacity, core[None], rows, own, other)
        spread = lax.all_to_all(pieces, "chip", split_axis=0, concat_axis=0, tiled=True)
        return regroup(groups, 2 * pairs, index, spread)

    pieces = lax.switch(
        branch[0],
        [functools.partial(exchange, size) for size in capacities],
        (picture_descriptors.reshape(halves), traded.reshape(halves), rows, index),
    )
    maps = all_pairs(pieces).reshape(chips, cores, *pieces.shape[1:])

    def move(array, step):
        return lax.ppermute(array, "quad", [(i, (i + step) % quads) for i in range(quads)])

    meta = jnp.stack([quad, pair_count[0]])
    partial = jnp.zeros((quads, 1, 8, slab), jnp.float32)
    for pair in range(pairs):
        query = maps[:, :, pair : pair + 1]
        before = move(query, 1)
        after = move(query, quads - 1)
        across = (move(before[: chips // 2], 1), move(after[chips // 2 :], quads - 1))
        partial = match(image_rows, multiplier, pair, meta, (before, *across, after), maps, partial)
    partial = lax.all_to_all(partial, "quad", split_axis=0, concat_axis=0, tiled=True)
    top = partial[:, :, 0]
    weight = jnp.exp2(top - jnp.max(top, axis=0, keepdims=True))
    total = jnp.sum(partial[:, :, 1] * weight, axis=0)
    fields = [jnp.sum(partial[:, :, 2 + field] * weight, axis=0) / total for field in range(3)]
    return jnp.where(in_use[None, :, None], jnp.stack(fields), 0.0).transpose(1, 0, 2)


def solution(mesh):
    pair_axis = ("chip", "core")
    split = Mesh(mesh.devices.reshape(-1, CORES, mesh.devices.shape[-1]), (*pair_axis, "quad"))
    return jax.shard_map(
        shards,
        mesh=split,
        in_specs=(P(pair_axis, "quad", None), P(), P(pair_axis), P(pair_axis), P(pair_axis)),
        out_specs=P(pair_axis, None, "quad"),
        check_vma=False,
    )
```

```python
import functools
import math

import jax
import jax.numpy as jnp
from jax import lax
from jax.experimental import pallas as pl
from jax.experimental.pallas import tpu as pltpu
from jax.sharding import Mesh
from jax.sharding import PartitionSpec as P

IMG_W = 64
TGT_G = 8
SHARPNESS_DIVISOR = 0.1
LOG2E = math.log2(math.e)
LANES = 128
CORES = 2
PLACE_BITS = 6
PLACES = 1 << PLACE_BITS
CAPACITIES = (6, 7, 8, 9, 10, 11, 12, 16)
ANY = pl.BlockSpec(memory_space=pl.ANY)
SMEM = pl.BlockSpec(memory_space=pltpu.SMEM)
VMEM = pl.BlockSpec(memory_space=pltpu.VMEM)


def announce_kernel(pairs, image_slot, group_images, pair_target, pair_count, out):
    lane = lax.broadcasted_iota(jnp.int32, out.shape, 2)
    message = jnp.full(out.shape, -1, jnp.int32)
    for entry in range(2 * pairs):
        pair = entry % pairs
        member = TGT_G + pair if entry < pairs else pair_target[pair]
        stored = jnp.where(pair < pair_count[0], image_slot[group_images[member]], -1)
        message = jnp.where(lane == entry, stored, message)
    out[...] = message


def announce(groups, image_slot, group_images, pair_target, pair_count):
    return pl.pallas_call(
        functools.partial(announce_kernel, pair_target.shape[0]),
        in_specs=[SMEM] * 4,
        out_specs=VMEM,
        out_shape=jax.ShapeDtypeStruct((groups, 1, LANES), jnp.int32),
    )(image_slot, group_images, pair_target, pair_count)


def plan_kernel(chip_rows, entries, capacities, chip, asked, index, rows, branch, requested, before):
    groups = asked.shape[0]
    table = asked[:, 0, :]
    lane = lax.broadcasted_iota(jnp.int32, (groups, LANES), 1)
    chips, locals_ = [], []
    count = jnp.zeros((LANES, LANES), jnp.float32)
    for entry in range(entries):
        stored = table[:, entry : entry + 1]
        chips.append(jnp.where(lax.div(stored, chip_rows) == lane, 1.0, 0.0) * jnp.where(stored >= 0, 1.0, 0.0))
        locals_.append(jnp.where(lax.rem(stored, chip_rows) == lane, 1.0, 0.0))
        count += lax.dot_general(
            chips[-1], locals_[-1], (((0,), (0,)), ((), ())), preferred_element_type=jnp.float32
        )
    flags = jnp.where(count > 0.0, 1.0, 0.0)
    first = lax.broadcasted_iota(jnp.int32, (LANES, LANES), 0)
    second = lax.broadcasted_iota(jnp.int32, (LANES, LANES), 1)
    earlier = jnp.dot(flags, jnp.where(first < second, 1.0, 0.0), preferred_element_type=jnp.float32)
    requested[...] = flags
    before[...] = earlier
    most = jnp.max(earlier + flags)
    choice = jnp.int32(0)
    for capacity in capacities[:-1]:
        choice += jnp.where(most > capacity, 1, 0)
    branch[0] = choice

    codes = jnp.zeros((groups, LANES), jnp.int32)
    for entry in range(entries):
        places = jnp.dot(chips[entry], earlier, preferred_element_type=jnp.float32) * locals_[entry]
        place = jnp.sum(places, axis=1, keepdims=True).astype(jnp.int32)
        stored = jnp.maximum(table[:, entry : entry + 1], 0)
        codes = jnp.where(lane == entry, lax.div(stored, chip_rows) * PLACES + place, codes)
    index[...] = codes

    mine = chip[0]
    slot = lax.broadcasted_iota(jnp.int32, (chip_rows, LANES), 0).astype(jnp.float32)
    along = lax.broadcasted_iota(jnp.int32, (chip_rows, LANES), 1).astype(jnp.float32)
    chosen = (requested[pl.ds(mine, 1), :] > 0.0) & (before[pl.ds(mine, 1), :] == slot)
    row = jnp.sum(jnp.where(chosen, along, 0.0), axis=1, keepdims=True)
    rows[...] = jnp.broadcast_to(row.astype(jnp.int32), rows.shape)


def plan(chip_rows, entries, capacities, chip, asked):
    groups = asked.shape[0]
    return pl.pallas_call(
        functools.partial(plan_kernel, chip_rows, entries, capacities),
        grid=(1,),
        in_specs=[SMEM, pl.BlockSpec(asked.shape, lambda step: (0, 0, 0))],
        out_specs=(
            pl.BlockSpec((groups, LANES), lambda step: (0, 0)),
            pl.BlockSpec((chip_rows, LANES), lambda step: (0, 0)),
            SMEM,
        ),
        out_shape=(
            jax.ShapeDtypeStruct((groups, LANES), jnp.int32),
            jax.ShapeDtypeStruct((chip_rows, LANES), jnp.int32),
            jax.ShapeDtypeStruct((1,), jnp.int32),
        ),
        scratch_shapes=[pltpu.VMEM((LANES, LANES), jnp.float32)] * 2,
    )(chip, asked)


def pick_kernel(core, rows, own, other, out, sems):
    images_dev = own.shape[0]
    capacity = out.shape[1]
    for slot in range(capacity):
        row = rows[slot, 0]
        local = lax.rem(row, images_dev)
        is_own = lax.div(row, images_dev) == core[0]

        @pl.when(is_own)
        def _():
            pltpu.make_async_copy(own.at[local, core[0]], out.at[:, slot], sems.at[slot]).start()

        @pl.when(jnp.logical_not(is_own))
        def _():
            pltpu.make_async_copy(other.at[local, core[0]], out.at[:, slot], sems.at[slot]).start()

    for slot in range(capacity):
        pltpu.make_async_copy(other.at[0, 0], out.at[:, slot], sems.at[slot]).wait()


def pick(capacity, core, rows, own, other):
    _, _, chips, piece, width = other.shape
    return pl.pallas_call(
        pick_kernel,
        in_specs=[SMEM, SMEM, ANY, ANY],
        out_specs=VMEM,
        out_shape=jax.ShapeDtypeStruct((chips, capacity, piece, width), other.dtype),
        scratch_shapes=[pltpu.SemaphoreType.DMA((capacity,))],
        compiler_params=pltpu.CompilerParams(vmem_limit_bytes=24 * 1024 * 1024),
    )(core, rows, own, other)


def regroup_kernel(index, spread, out):
    groups, entries = out.shape[:2]

    def step(group, carry):
        for entry in range(entries):
            code = index[group, entry]
            out[group, entry] = spread[code >> PLACE_BITS, code & (PLACES - 1)]
        return carry

    lax.fori_loop(0, groups, step, 0, unroll=8)


def regroup(groups, entries, index, spread):
    return pl.pallas_call(
        regroup_kernel,
        in_specs=[SMEM, VMEM],
        out_specs=VMEM,
        out_shape=jax.ShapeDtypeStruct((groups, entries, *spread.shape[2:]), spread.dtype),
        compiler_params=pltpu.CompilerParams(vmem_limit_bytes=24 * 1024 * 1024),
    )(index, spread)


def match_kernel(image_rows, multiplier, pair, meta, maps, q1, q2a, q2b, q3, *refs):
    *earlier, out0, out1, out2, out3, scores, column = refs
    outs = (out0, out1, out2, out3)
    quad = meta[0]
    chips, cores, entries, piece, width = maps.shape
    target_entry = entries // 2 + pair
    part = chips * piece
    slab = cores * part
    quads = len(outs)
    for old, new in zip(earlier, outs):
        new[0:pair] = old[...]

    @pl.when(pair < meta[1])
    def _():
        for row in range(cores):
            rows = maps[:, row, target_entry].reshape(part, width)
            blocks = ((0, 0, maps, pair), (1, 0, q1, 0), (2, 0, q2a, 0), (2, q2a.shape[0], q2b, 0), (3, 0, q3, 0))
            for step, skip, query, entry in blocks:
                tokens = query.shape[0] * piece
                for core in range(cores):
                    start = step * slab + core * part + skip * piece
                    scores[row * part : (row + 1) * part, start : start + tokens] = (
                        lax.dot_general(
                            rows, query[:, core, entry].reshape(tokens, width), (((1,), (1,)), ((), ())),
                            preferred_element_type=jnp.float32,
                        )
                        * multiplier
                    )

        def rows_step(index, carry):
            block = pl.ds(pl.multiple_of(index * 32, 32), 32)
            top = jnp.max(scores[block, :], axis=1, keepdims=True)
            powers = jnp.exp2(scores[block, :] - top)
            column[block, :] = powers * (1.0 / jnp.sum(powers, axis=1, keepdims=True))
            return carry

        lax.fori_loop(0, slab // 32, rows_step, 0, unroll=4)

        bands = slab // IMG_W
        along = lax.broadcasted_iota(jnp.int32, (IMG_W, LANES), 0).astype(jnp.float32)
        coord_x = (2.0 * along + 1.0) / IMG_W - 1.0
        first_row = quad * bands
        for step in range(quads):
            out = outs[step]

            def lanes_step(index, carry, step=step, out=out):
                lanes = pl.ds(pl.multiple_of(step * slab + index * LANES, LANES), LANES)
                top = jnp.max(scores[:, lanes], axis=0, keepdims=True)
                total = jnp.zeros((8, LANES), jnp.float32)
                weighted_y = jnp.zeros((8, LANES), jnp.float32)
                mutual = jnp.zeros((8, LANES), jnp.float32)
                folded = jnp.zeros((IMG_W, LANES), jnp.float32)
                for band in range(bands):
                    piece = slice(band * IMG_W, (band + 1) * IMG_W)
                    powers = jnp.exp2(scores[piece, lanes] - top)
                    folded += powers
                    part = jnp.sum(powers.reshape(IMG_W // 8, 8, LANES), axis=0)
                    total += part
                    coord_y = (2.0 * (first_row + band).astype(jnp.float32) + 1.0) / image_rows - 1.0
                    weighted_y += part * coord_y
                    mutual += jnp.sum((powers * column[piece, lanes]).reshape(IMG_W // 8, 8, LANES), axis=0)
                place = pl.ds(pl.multiple_of(index * LANES, LANES), LANES)
                out[pair, 0:1, place] = top
                out[pair, 1:2, place] = jnp.sum(total, axis=0, keepdims=True)
                out[pair, 2:3, place] = jnp.sum(folded * coord_x, axis=0, keepdims=True)
                out[pair, 3:4, place] = jnp.sum(weighted_y, axis=0, keepdims=True)
                out[pair, 4:5, place] = jnp.sum(mutual, axis=0, keepdims=True)
                return carry

            lax.fori_loop(0, slab // LANES, lanes_step, 0, unroll=4)


def match(image_rows, multiplier, pair, meta, queries, maps, earlier):
    chips, cores, _, piece, width = maps.shape
    quads = len(queries)
    slab = chips * cores * piece
    return pl.pallas_call(
        functools.partial(match_kernel, image_rows, multiplier, pair),
        in_specs=[SMEM] + [VMEM] * (1 + len(queries) + len(earlier)),
        out_specs=[VMEM] * quads,
        out_shape=[jax.ShapeDtypeStruct((pair + 1, 8, slab), jnp.float32)] * quads,
        scratch_shapes=[pltpu.VMEM((slab, quads * slab), jnp.float32)] * 2,
        compiler_params=pltpu.CompilerParams(vmem_limit_bytes=32 * 1024 * 1024),
        cost_estimate=pl.CostEstimate(
            flops=2 * slab * slab * quads * width, bytes_accessed=2 << 20, transcendentals=2 << 20
        ),
    )(meta, maps, *queries, *earlier)


def shards(picture_descriptors, image_slot, group_images, pair_target, pair_count):
    chips = lax.axis_size("chip")
    cores = lax.axis_size("core")
    quads = lax.axis_size("quad")
    groups = chips * cores
    chip = lax.axis_index("chip").astype(jnp.int32)
    core = lax.axis_index("core").astype(jnp.int32)
    quad = lax.axis_index("quad").astype(jnp.int32)
    images_dev, slab, width = picture_descriptors.shape
    pairs = pair_target.shape[0]
    chip_rows = images_dev * cores
    image_rows = slab * quads // IMG_W
    multiplier = LOG2E / (width * SHARPNESS_DIVISOR)

    def all_pairs(array):
        return lax.all_to_all(array, ("chip", "core"), split_axis=0, concat_axis=0, tiled=True)

    traded = lax.ppermute(picture_descriptors, "core", [(i, (i + 1) % cores) for i in range(cores)])

    asked = all_pairs(announce(groups, image_slot, group_images, pair_target, pair_count))

    capacities = [size for size in CAPACITIES if size < chip_rows] + [chip_rows]
    index, rows, branch = plan(chip_rows, 2 * pairs, capacities, chip[None], asked)
    halves = (images_dev, cores, chips, slab // groups, width)

    def exchange(capacity, operands):
        own, other, rows, index = operands
        pieces = pick(capacity, core[None], rows, own, other)
        spread = lax.all_to_all(pieces, "chip", split_axis=0, concat_axis=0, tiled=True)
        return regroup(groups, 2 * pairs, index, spread)

    pieces = lax.switch(
        branch[0],
        [functools.partial(exchange, size) for size in capacities],
        (picture_descriptors.reshape(halves), traded.reshape(halves), rows, index),
    )
    maps = all_pairs(pieces).reshape(chips, cores, *pieces.shape[1:])

    def move(array, step):
        return lax.ppermute(array, "quad", [(i, (i + step) % quads) for i in range(quads)])

    meta = jnp.stack([quad, pair_count[0]])
    partials = []
    for pair in range(pairs):
        query = maps[:, :, pair : pair + 1]
        before = move(query, 1)
        after = move(query, quads - 1)
        across = (move(before[: chips // 2], 1), move(after[chips // 2 :], quads - 1))
        partials = match(image_rows, multiplier, pair, meta, (before, *across, after), maps, partials)
    partial = jnp.stack([partials[0]] + [move(partials[step], quads - step) for step in range(1, quads)])
    top = partial[:, :, 0]
    weight = jnp.exp2(top - jnp.max(top, axis=0, keepdims=True))
    total = jnp.sum(partial[:, :, 1] * weight, axis=0)
    fields = [jnp.sum(partial[:, :, 2 + field] * weight, axis=0) / total for field in range(3)]
    in_use = jnp.arange(pairs, dtype=jnp.int32) < pair_count[0]
    return jnp.where(in_use[None, :, None], jnp.stack(fields), 0.0).transpose(1, 0, 2)


def solution(mesh):
    pair_axis = ("chip", "core")
    split = Mesh(mesh.devices.reshape(-1, CORES, mesh.devices.shape[-1]), (*pair_axis, "quad"))
    return jax.shard_map(
        shards,
        mesh=split,
        in_specs=(P(pair_axis, "quad", None), P(), P(pair_axis), P(pair_axis), P(pair_axis)),
        out_specs=P(pair_axis, None, "quad"),
        check_vma=False,
    )
```

```python
import functools

import jax
import jax.numpy as jnp
from jax import lax
from jax.experimental import pallas as pl
from jax.experimental.pallas import tpu as pltpu
from jax.sharding import Mesh
from jax.sharding import PartitionSpec as P

IMG_W = 64
TGT_G = 8
SHARPNESS_DIVISOR = 0.1
LANES = 128
CORES = 2
PLACE_BITS = 6
PLACES = 1 << PLACE_BITS
CAPACITIES = (6, 7, 8, 9, 10, 11, 12, 16)
ANY = pl.BlockSpec(memory_space=pl.ANY)
SMEM = pl.BlockSpec(memory_space=pltpu.SMEM)
VMEM = pl.BlockSpec(memory_space=pltpu.VMEM)


def announce_kernel(pairs, image_slot, group_images, pair_target, pair_count, out):
    lane = lax.broadcasted_iota(jnp.int32, out.shape, 2)
    message = jnp.full(out.shape, -1, jnp.int32)
    for entry in range(2 * pairs):
        pair = entry % pairs
        member = TGT_G + pair if entry < pairs else pair_target[pair]
        stored = jnp.where(pair < pair_count[0], image_slot[group_images[member]], -1)
        message = jnp.where(lane == entry, stored, message)
    out[...] = message


def announce(groups, image_slot, group_images, pair_target, pair_count):
    return pl.pallas_call(
        functools.partial(announce_kernel, pair_target.shape[0]),
        in_specs=[SMEM] * 4,
        out_specs=VMEM,
        out_shape=jax.ShapeDtypeStruct((groups, 1, LANES), jnp.int32),
    )(image_slot, group_images, pair_target, pair_count)


def plan_kernel(chip_rows, entries, capacities, chip, asked, index, rows, branch, requested, before):
    groups = asked.shape[0]
    table = asked[:, 0, :]
    lane = lax.broadcasted_iota(jnp.int32, (groups, LANES), 1)
    chips, locals_ = [], []
    count = jnp.zeros((LANES, LANES), jnp.float32)
    for entry in range(entries):
        stored = table[:, entry : entry + 1]
        chips.append(jnp.where(lax.div(stored, chip_rows) == lane, 1.0, 0.0) * jnp.where(stored >= 0, 1.0, 0.0))
        locals_.append(jnp.where(lax.rem(stored, chip_rows) == lane, 1.0, 0.0))
        count += lax.dot_general(
            chips[-1], locals_[-1], (((0,), (0,)), ((), ())), preferred_element_type=jnp.float32
        )
    flags = jnp.where(count > 0.0, 1.0, 0.0)
    first = lax.broadcasted_iota(jnp.int32, (LANES, LANES), 0)
    second = lax.broadcasted_iota(jnp.int32, (LANES, LANES), 1)
    earlier = jnp.dot(flags, jnp.where(first < second, 1.0, 0.0), preferred_element_type=jnp.float32)
    requested[...] = flags
    before[...] = earlier
    most = jnp.max(earlier + flags)
    choice = jnp.int32(0)
    for capacity in capacities[:-1]:
        choice += jnp.where(most > capacity, 1, 0)
    branch[0] = choice

    codes = jnp.zeros((groups, LANES), jnp.int32)
    for entry in range(entries):
        places = jnp.dot(chips[entry], earlier, preferred_element_type=jnp.float32) * locals_[entry]
        place = jnp.sum(places, axis=1, keepdims=True).astype(jnp.int32)
        stored = jnp.maximum(table[:, entry : entry + 1], 0)
        codes = jnp.where(lane == entry, lax.div(stored, chip_rows) * PLACES + place, codes)
    index[...] = codes

    mine = chip[0]
    slot = lax.broadcasted_iota(jnp.int32, (chip_rows, LANES), 0).astype(jnp.float32)
    along = lax.broadcasted_iota(jnp.int32, (chip_rows, LANES), 1).astype(jnp.float32)
    chosen = (requested[pl.ds(mine, 1), :] > 0.0) & (before[pl.ds(mine, 1), :] == slot)
    row = jnp.sum(jnp.where(chosen, along, 0.0), axis=1, keepdims=True)
    rows[...] = jnp.broadcast_to(row.astype(jnp.int32), rows.shape)


def plan(chip_rows, entries, capacities, chip, asked):
    groups = asked.shape[0]
    return pl.pallas_call(
        functools.partial(plan_kernel, chip_rows, entries, capacities),
        grid=(1,),
        in_specs=[SMEM, pl.BlockSpec(asked.shape, lambda step: (0, 0, 0))],
        out_specs=(
            pl.BlockSpec((groups, LANES), lambda step: (0, 0)),
            pl.BlockSpec((chip_rows, LANES), lambda step: (0, 0)),
            SMEM,
        ),
        out_shape=(
            jax.ShapeDtypeStruct((groups, LANES), jnp.int32),
            jax.ShapeDtypeStruct((chip_rows, LANES), jnp.int32),
            jax.ShapeDtypeStruct((1,), jnp.int32),
        ),
        scratch_shapes=[pltpu.VMEM((LANES, LANES), jnp.float32)] * 2,
    )(chip, asked)


def pick_kernel(core, rows, own, other, out, sems):
    images_dev = own.shape[0]
    capacity = out.shape[1]
    for slot in range(capacity):
        row = rows[slot, 0]
        local = lax.rem(row, images_dev)
        is_own = lax.div(row, images_dev) == core[0]

        @pl.when(is_own)
        def _():
            pltpu.make_async_copy(own.at[local, core[0]], out.at[:, slot], sems.at[slot]).start()

        @pl.when(jnp.logical_not(is_own))
        def _():
            pltpu.make_async_copy(other.at[local, core[0]], out.at[:, slot], sems.at[slot]).start()

    for slot in range(capacity):
        pltpu.make_async_copy(other.at[0, 0], out.at[:, slot], sems.at[slot]).wait()


def pick(capacity, core, rows, own, other):
    _, _, chips, piece, width = other.shape
    return pl.pallas_call(
        pick_kernel,
        in_specs=[SMEM, SMEM, ANY, ANY],
        out_specs=VMEM,
        out_shape=jax.ShapeDtypeStruct((chips, capacity, piece, width), other.dtype),
        scratch_shapes=[pltpu.SemaphoreType.DMA((capacity,))],
        compiler_params=pltpu.CompilerParams(vmem_limit_bytes=24 * 1024 * 1024),
    )(core, rows, own, other)


def regroup_kernel(index, spread, out):
    groups, entries = out.shape[:2]

    def step(group, carry):
        for entry in range(entries):
            code = index[group, entry]
            out[group, entry] = spread[code >> PLACE_BITS, code & (PLACES - 1)]
        return carry

    lax.fori_loop(0, groups, step, 0, unroll=8)


def regroup(groups, entries, index, spread):
    return pl.pallas_call(
        regroup_kernel,
        in_specs=[SMEM, VMEM],
        out_specs=VMEM,
        out_shape=jax.ShapeDtypeStruct((groups, entries, *spread.shape[2:]), spread.dtype),
        compiler_params=pltpu.CompilerParams(vmem_limit_bytes=24 * 1024 * 1024),
    )(index, spread)


def score_kernel(image_rows, multiplier, pair, meta, maps, near_query, near_target, products, rows, columns, scores, stats):
    chips, cores, entries, piece, width = maps.shape
    part = chips * piece
    slab = cores * part
    targets = ((maps, entries // 2 + pair), (near_target, 0))
    queries = ((maps, pair), (near_query, 0))

    @pl.when(pair < meta[1])
    def _():
        for row in range(2 * cores):
            target, entry = targets[row // cores]
            tokens = target[:, row % cores, entry].reshape(part, width)
            for column in range(2 * cores):
                query, entry = queries[column // cores]
                scores[row * part : (row + 1) * part, column * part : (column + 1) * part] = (
                    lax.dot_general(
                        tokens, query[:, column % cores, entry].reshape(part, width), (((1,), (1,)), ((), ())),
                        preferred_element_type=jnp.float32,
                    )
                    * multiplier
                )

        first_lane = lax.broadcasted_iota(jnp.int32, (64, LANES), 1) == 0

        def rows_step(index, carry):
            block = pl.ds(pl.multiple_of(index * 64, 64), 64)
            top = jnp.max(scores[block, :], axis=1, keepdims=True)
            powers = jnp.exp(scores[block, :] - top)
            products[block, :] = powers
            stats[block, :] = jnp.where(first_lane, top, jnp.sum(powers, axis=1, keepdims=True))
            return carry

        lax.fori_loop(0, 2 * slab // 64, rows_step, 0, unroll=4)
        for start in range(0, 2 * slab, LANES):
            columns[:, start : start + LANES] = stats[start : start + LANES, :].T[0:8, :]

        bands = slab // IMG_W
        along = lax.broadcasted_iota(jnp.int32, (IMG_W, LANES), 0).astype(jnp.float32)
        coord_x = (2.0 * along + 1.0) / IMG_W - 1.0

        def lanes_step(index, carry):
            lanes = pl.ds(pl.multiple_of(index * LANES, LANES), LANES)
            top = jnp.max(scores[:, lanes], axis=0, keepdims=True)
            total = jnp.zeros((8, LANES), jnp.float32)
            weighted_y = jnp.zeros((8, LANES), jnp.float32)
            folded = jnp.zeros((IMG_W, LANES), jnp.float32)
            for band in range(2 * bands):
                block = slice(band * IMG_W, (band + 1) * IMG_W)
                powers = jnp.exp(scores[block, lanes] - top)
                products[block, lanes] *= powers
                folded += powers
                sums = jnp.sum(powers.reshape(IMG_W // 8, 8, LANES), axis=0)
                total += sums
                image_row = meta[2 + band // bands] * bands + band % bands
                weighted_y += sums * ((2.0 * image_row.astype(jnp.float32) + 1.0) / image_rows - 1.0)
            rows[0:1, lanes] = top
            rows[1:2, lanes] = jnp.sum(total, axis=0, keepdims=True)
            rows[2:3, lanes] = jnp.sum(folded * coord_x, axis=0, keepdims=True)
            rows[3:4, lanes] = jnp.sum(weighted_y, axis=0, keepdims=True)
            return carry

        lax.fori_loop(0, 2 * slab // LANES, lanes_step, 0, unroll=4)


def score(image_rows, multiplier, pair, meta, maps, near_query, near_target):
    chips, cores, _, piece, width = maps.shape
    tokens = 2 * chips * cores * piece
    return pl.pallas_call(
        functools.partial(score_kernel, image_rows, multiplier, pair),
        in_specs=[SMEM] + [VMEM] * 3,
        out_specs=[VMEM] * 3,
        out_shape=[
            jax.ShapeDtypeStruct((tokens, tokens), jnp.float32),
            jax.ShapeDtypeStruct((8, tokens), jnp.float32),
            jax.ShapeDtypeStruct((8, tokens), jnp.float32),
        ],
        scratch_shapes=[pltpu.VMEM((tokens, tokens), jnp.float32), pltpu.VMEM((tokens, LANES), jnp.float32)],
        compiler_params=pltpu.CompilerParams(vmem_limit_bytes=20 * 1024 * 1024),
        cost_estimate=pl.CostEstimate(
            flops=2 * tokens * tokens * width, bytes_accessed=2 << 20, transcendentals=2 << 20
        ),
    )(meta, maps, near_query, near_target)


def mutual_kernel(pairs, meta, *refs):
    products, rows, columns, others = (refs[pairs * kind : pairs * (kind + 1)] for kind in range(4))
    kept, sent, weights = refs[4 * pairs :]
    tokens = weights.shape[0]
    slab = tokens // 2
    for pair in range(pairs):

        @pl.when(pair < meta[1])
        def _():
            for start in range(0, tokens, LANES):
                here = slice(start, start + LANES)
                there = slice((start + slab) % tokens, (start + slab) % tokens + LANES)
                top = columns[pair][0:1, here]
                other_top = others[pair][0:1, there]
                highest = jnp.maximum(top, other_top)
                scale = jnp.exp(top - highest)
                total = columns[pair][1:2, here] * scale + others[pair][1:2, there] * jnp.exp(other_top - highest)
                weights[here, :] = jnp.broadcast_to(scale / total, (LANES, LANES)).T

            for half, out in enumerate((kept, sent)):
                out[pair, 0:4, :] = rows[pair][0:4, half * slab : (half + 1) * slab]
                for start in range(0, slab, LANES):
                    lanes = slice(half * slab + start, half * slab + start + LANES)
                    mutual = jnp.zeros((64, LANES), jnp.float32)
                    for row in range(0, tokens, 64):
                        mutual += products[pair][row : row + 64, lanes] * weights[row : row + 64, :]
                    out[pair, 4:5, start : start + LANES] = jnp.sum(mutual, axis=0, keepdims=True)


def mutual(meta, products, rows, columns, others):
    pairs = len(products)
    tokens = products[0].shape[0]
    shape = jax.ShapeDtypeStruct((pairs, 8, tokens // 2), jnp.float32)
    return pl.pallas_call(
        functools.partial(mutual_kernel, pairs),
        in_specs=[SMEM] + [VMEM] * (4 * pairs),
        out_specs=[VMEM] * 2,
        out_shape=[shape] * 2,
        scratch_shapes=[pltpu.VMEM((tokens, LANES), jnp.float32)],
        compiler_params=pltpu.CompilerParams(vmem_limit_bytes=20 * 1024 * 1024),
    )(meta, *products, *rows, *columns, *others)


def shards(picture_descriptors, image_slot, group_images, pair_target, pair_count):
    chips = lax.axis_size("chip")
    cores = lax.axis_size("core")
    quads = lax.axis_size("quad")
    groups = chips * cores
    chip = lax.axis_index("chip").astype(jnp.int32)
    core = lax.axis_index("core").astype(jnp.int32)
    quad = lax.axis_index("quad").astype(jnp.int32)
    images_dev, slab, width = picture_descriptors.shape
    pairs = pair_target.shape[0]
    chip_rows = images_dev * cores
    image_rows = slab * quads // IMG_W
    multiplier = 1.0 / (width * SHARPNESS_DIVISOR)

    def all_pairs(array):
        return lax.all_to_all(array, ("chip", "core"), split_axis=0, concat_axis=0, tiled=True)

    traded = lax.ppermute(picture_descriptors, "core", [(i, (i + 1) % cores) for i in range(cores)])

    asked = all_pairs(announce(groups, image_slot, group_images, pair_target, pair_count))

    capacities = [size for size in CAPACITIES if size < chip_rows] + [chip_rows]
    index, listed, branch = plan(chip_rows, 2 * pairs, capacities, chip[None], asked)
    halves = (images_dev, cores, chips, slab // groups, width)

    def exchange(capacity, operands):
        own, other, rows, index = operands
        pieces = pick(capacity, core[None], rows, own, other)
        spread = lax.all_to_all(pieces, "chip", split_axis=0, concat_axis=0, tiled=True)
        return regroup(groups, 2 * pairs, index, spread)

    pieces = lax.switch(
        branch[0],
        [functools.partial(exchange, size) for size in capacities],
        (picture_descriptors.reshape(halves), traded.reshape(halves), listed, index),
    )
    maps = all_pairs(pieces).reshape(chips, cores, *pieces.shape[1:])

    def trade(array, flip):
        return lax.ppermute(array, "quad", [(i, i ^ flip) for i in range(quads)])

    query_flip, target_flip = 1, quads - 1
    meta = jnp.stack([quad, pair_count[0], quad, quad ^ target_flip])
    products, rows, columns = [], [], []
    for pair in range(pairs):
        near_query = trade(maps[:, :, pair : pair + 1], query_flip)
        near_target = trade(maps[:, :, pairs + pair : pairs + pair + 1], target_flip)
        parts = score(image_rows, multiplier, pair, meta, maps, near_query, near_target)
        for kept, part in zip((products, rows, columns), parts):
            kept.append(part)
    others = [trade(column, target_flip) for column in columns]
    kept, sent = mutual(meta, products, rows, columns, others)
    partial = jnp.stack([kept, trade(sent, query_flip)])
    top = partial[:, :, 0]
    weight = jnp.exp(top - jnp.max(top, axis=0, keepdims=True))
    total = jnp.sum(partial[:, :, 1] * weight, axis=0)
    fields = [jnp.sum(partial[:, :, 2 + field] * weight, axis=0) / total for field in range(3)]
    in_use = jnp.arange(pairs, dtype=jnp.int32) < pair_count[0]
    return jnp.where(in_use[None, :, None], jnp.stack(fields), 0.0).transpose(1, 0, 2)


def solution(mesh):
    pair_axis = ("chip", "core")
    split = Mesh(mesh.devices.reshape(-1, CORES, mesh.devices.shape[-1]), (*pair_axis, "quad"))
    return jax.shard_map(
        shards,
        mesh=split,
        in_specs=(P(pair_axis, "quad", None), P(), P(pair_axis), P(pair_axis), P(pair_axis)),
        out_specs=P(pair_axis, None, "quad"),
        check_vma=False,
    )
```

```python
import functools

import jax
import jax.numpy as jnp
from jax import lax
from jax.experimental import pallas as pl
from jax.experimental.pallas import tpu as pltpu
from jax.sharding import Mesh
from jax.sharding import PartitionSpec as P

IMG_W = 64
TGT_G = 8
SHARPNESS_DIVISOR = 0.1
LANES = 128
CORES = 2
PLACE_BITS = 6
PLACES = 1 << PLACE_BITS
CAPACITIES = (6, 7, 8, 9, 10, 11, 12, 16)
ANY = pl.BlockSpec(memory_space=pl.ANY)
SMEM = pl.BlockSpec(memory_space=pltpu.SMEM)
VMEM = pl.BlockSpec(memory_space=pltpu.VMEM)


def announce_kernel(pairs, image_slot, group_images, pair_target, pair_count, out):
    lane = lax.broadcasted_iota(jnp.int32, out.shape, 2)
    message = jnp.full(out.shape, -1, jnp.int32)
    for entry in range(2 * pairs):
        pair = entry % pairs
        member = TGT_G + pair if entry < pairs else pair_target[pair]
        stored = jnp.where(pair < pair_count[0], image_slot[group_images[member]], -1)
        message = jnp.where(lane == entry, stored, message)
    out[...] = message


def announce(groups, image_slot, group_images, pair_target, pair_count):
    return pl.pallas_call(
        functools.partial(announce_kernel, pair_target.shape[0]),
        in_specs=[SMEM] * 4,
        out_specs=VMEM,
        out_shape=jax.ShapeDtypeStruct((groups, 1, LANES), jnp.int32),
    )(image_slot, group_images, pair_target, pair_count)


def plan_kernel(chip_rows, entries, capacities, chip, asked, index, rows, branch):
    groups = asked.shape[0]
    table = asked[...].T
    chips_of, rows_of, stored_of = [], [], []
    wide = lax.broadcasted_iota(jnp.int32, (chip_rows, groups), 0)
    count = jnp.zeros((chip_rows, chip_rows), jnp.float32)
    for entry in range(entries):
        stored = table[entry : entry + 1, :]
        valid = jnp.where(stored >= 0, 1.0, 0.0)
        stored_of.append(jnp.maximum(stored, 0))
        chips_of.append(jnp.where(lax.div(stored_of[-1], chip_rows) == wide, valid, 0.0))
        rows_of.append(jnp.where(lax.rem(stored_of[-1], chip_rows) == wide, 1.0, 0.0))
        count += lax.dot_general(
            rows_of[-1], chips_of[-1], (((1,), (1,)), ((), ())), preferred_element_type=jnp.float32
        )
    flags = jnp.where(count > 0.0, 1.0, 0.0)
    first = lax.broadcasted_iota(jnp.int32, (chip_rows, chip_rows), 0)
    second = lax.broadcasted_iota(jnp.int32, (chip_rows, chip_rows), 1)
    earlier = jnp.dot(jnp.where(second < first, 1.0, 0.0), flags, preferred_element_type=jnp.float32)
    most = jnp.max(earlier + flags)
    choice = jnp.int32(0)
    for capacity in capacities[:-1]:
        choice += jnp.where(most > capacity, 1, 0)
    branch[0] = choice

    here = second == chip[0]
    my_flag = jnp.max(jnp.where(here, flags, 0.0), axis=1, keepdims=True)
    my_place = jnp.max(jnp.where(here, earlier, 0.0), axis=1, keepdims=True)
    slot = lax.broadcasted_iota(jnp.int32, (chip_rows, LANES), 1).astype(jnp.float32)
    row = lax.broadcasted_iota(jnp.int32, (chip_rows, LANES), 0).astype(jnp.float32)
    chosen = jnp.where((my_flag > 0.0) & (my_place == slot), row, 0.0)
    rows[...] = jnp.broadcast_to(jnp.sum(chosen, axis=0, keepdims=True), rows.shape).astype(jnp.int32)

    for entry in range(entries):
        places = jnp.dot(earlier, chips_of[entry], preferred_element_type=jnp.float32) * rows_of[entry]
        place = jnp.sum(places, axis=0, keepdims=True).astype(jnp.int32)
        index[entry : entry + 1, :] = lax.div(stored_of[entry], chip_rows) * PLACES + place


def plan(chip_rows, entries, capacities, chip, asked):
    groups = asked.shape[0]
    return pl.pallas_call(
        functools.partial(plan_kernel, chip_rows, entries, capacities),
        in_specs=[SMEM, VMEM],
        out_specs=(VMEM, VMEM, SMEM),
        out_shape=(
            jax.ShapeDtypeStruct((8, groups), jnp.int32),
            jax.ShapeDtypeStruct((8, LANES), jnp.int32),
            jax.ShapeDtypeStruct((1,), jnp.int32),
        ),
    )(chip, asked)


def pick_kernel(core, rows, own, other, out, sems):
    images_dev = own.shape[0]
    capacity = out.shape[1]
    for slot in range(capacity):
        row = rows[0, slot]
        local = lax.rem(row, images_dev)
        is_own = lax.div(row, images_dev) == core[0]

        @pl.when(is_own)
        def _():
            pltpu.make_async_copy(own.at[local, core[0]], out.at[:, slot], sems.at[slot]).start()

        @pl.when(jnp.logical_not(is_own))
        def _():
            pltpu.make_async_copy(other.at[local, core[0]], out.at[:, slot], sems.at[slot]).start()

    for slot in range(capacity):
        pltpu.make_async_copy(other.at[0, 0], out.at[:, slot], sems.at[slot]).wait()


def pick(capacity, core, rows, own, other):
    _, _, chips, piece, width = other.shape
    return pl.pallas_call(
        pick_kernel,
        in_specs=[SMEM, SMEM, ANY, ANY],
        out_specs=VMEM,
        out_shape=jax.ShapeDtypeStruct((chips, capacity, piece, width), other.dtype),
        scratch_shapes=[pltpu.SemaphoreType.DMA((capacity,))],
        compiler_params=pltpu.CompilerParams(vmem_limit_bytes=24 * 1024 * 1024),
    )(core, rows, own, other)


def regroup_kernel(index, spread, out):
    groups, entries = out.shape[:2]

    def step(group, carry):
        for entry in range(entries):
            code = index[entry, group]
            out[group, entry] = spread[code >> PLACE_BITS, code & (PLACES - 1)]
        return carry

    lax.fori_loop(0, groups, step, 0, unroll=8)


def regroup(groups, entries, index, spread):
    return pl.pallas_call(
        regroup_kernel,
        in_specs=[SMEM, VMEM],
        out_specs=VMEM,
        out_shape=jax.ShapeDtypeStruct((groups, entries, *spread.shape[2:]), spread.dtype),
        compiler_params=pltpu.CompilerParams(vmem_limit_bytes=24 * 1024 * 1024),
    )(index, spread)


def score_kernel(image_rows, multiplier, pair, meta, maps, near_query, near_target, *refs):
    *earlier, products, rows, columns, scores, stats = refs
    for previous in earlier:
        columns[0:pair] = previous[...]
    chips, cores, entries, piece, width = maps.shape
    part = chips * piece
    slab = cores * part
    targets = ((maps, entries // 2 + pair), (near_target, 0))
    queries = ((maps, pair), (near_query, 0))

    @pl.when(pair < meta[1])
    def _():
        for row in range(2 * cores):
            target, entry = targets[row // cores]
            tokens = target[:, row % cores, entry].reshape(part, width)
            for column in range(2 * cores):
                query, entry = queries[column // cores]
                scores[row * part : (row + 1) * part, column * part : (column + 1) * part] = (
                    lax.dot_general(
                        tokens, query[:, column % cores, entry].reshape(part, width), (((1,), (1,)), ((), ())),
                        preferred_element_type=jnp.float32,
                    )
                    * multiplier
                )

        first_lane = lax.broadcasted_iota(jnp.int32, (64, LANES), 1) == 0

        def rows_step(index, carry):
            block = pl.ds(pl.multiple_of(index * 64, 64), 64)
            top = jnp.max(scores[block, :], axis=1, keepdims=True)
            powers = jnp.exp(scores[block, :] - top)
            products[block, :] = powers
            stats[block, :] = jnp.where(first_lane, top, jnp.sum(powers, axis=1, keepdims=True))
            return carry

        lax.fori_loop(0, 2 * slab // 64, rows_step, 0, unroll=16)
        for start in range(0, 2 * slab, LANES):
            columns[pair, :, start : start + LANES] = stats[start : start + LANES, :].T[0:8, :]

        bands = slab // IMG_W
        along = lax.broadcasted_iota(jnp.int32, (IMG_W, LANES), 0).astype(jnp.float32)
        coord_x = (2.0 * along + 1.0) / IMG_W - 1.0

        def lanes_step(index, carry):
            lanes = pl.ds(pl.multiple_of(index * LANES, LANES), LANES)
            top = jnp.max(scores[:, lanes], axis=0, keepdims=True)
            total = jnp.zeros((8, LANES), jnp.float32)
            weighted_y = jnp.zeros((8, LANES), jnp.float32)
            folded = jnp.zeros((IMG_W, LANES), jnp.float32)
            for band in range(2 * bands):
                block = slice(band * IMG_W, (band + 1) * IMG_W)
                powers = jnp.exp(scores[block, lanes] - top)
                products[block, lanes] *= powers
                folded += powers
                sums = jnp.sum(powers.reshape(IMG_W // 8, 8, LANES), axis=0)
                total += sums
                image_row = meta[2 + band // bands] * bands + band % bands
                weighted_y += sums * ((2.0 * image_row.astype(jnp.float32) + 1.0) / image_rows - 1.0)
            rows[0:1, lanes] = top
            rows[1:2, lanes] = jnp.sum(total, axis=0, keepdims=True)
            rows[2:3, lanes] = jnp.sum(folded * coord_x, axis=0, keepdims=True)
            rows[3:4, lanes] = jnp.sum(weighted_y, axis=0, keepdims=True)
            return carry

        lax.fori_loop(0, 2 * slab // LANES, lanes_step, 0, unroll=8)


def score(image_rows, multiplier, pair, meta, maps, near_query, near_target, earlier):
    chips, cores, _, piece, width = maps.shape
    tokens = 2 * chips * cores * piece
    return pl.pallas_call(
        functools.partial(score_kernel, image_rows, multiplier, pair),
        in_specs=[SMEM] + [VMEM] * (3 + len(earlier)),
        out_specs=[VMEM] * 3,
        out_shape=[
            jax.ShapeDtypeStruct((tokens, tokens), jnp.float32),
            jax.ShapeDtypeStruct((8, tokens), jnp.float32),
            jax.ShapeDtypeStruct((pair + 1, 8, tokens), jnp.float32),
        ],
        scratch_shapes=[pltpu.VMEM((tokens, tokens), jnp.float32), pltpu.VMEM((tokens, LANES), jnp.float32)],
        compiler_params=pltpu.CompilerParams(vmem_limit_bytes=20 * 1024 * 1024),
        cost_estimate=pl.CostEstimate(
            flops=2 * tokens * tokens * width, bytes_accessed=2 << 20, transcendentals=2 << 20
        ),
    )(meta, maps, near_query, near_target, *earlier)


def mutual_kernel(pairs, meta, *refs):
    products, rows = refs[:pairs], refs[pairs : 2 * pairs]
    columns, others, kept, sent, weights = refs[2 * pairs :]
    tokens = weights.shape[0]
    slab = tokens // 2
    for pair in range(pairs):

        @pl.when(pair < meta[1])
        def _():
            for start in range(0, tokens, LANES):
                here = slice(start, start + LANES)
                there = slice((start + slab) % tokens, (start + slab) % tokens + LANES)
                top = columns[pair, 0:1, here]
                other_top = others[pair, 0:1, there]
                highest = jnp.maximum(top, other_top)
                scale = jnp.exp(top - highest)
                total = columns[pair, 1:2, here] * scale + others[pair, 1:2, there] * jnp.exp(other_top - highest)
                weights[here, :] = jnp.broadcast_to(scale / total, (LANES, LANES)).T

            for half, out in enumerate((kept, sent)):
                out[pair, 0:4, :] = rows[pair][0:4, half * slab : (half + 1) * slab]
                for start in range(0, slab, LANES):
                    lanes = slice(half * slab + start, half * slab + start + LANES)
                    mutual = jnp.zeros((64, LANES), jnp.float32)
                    for row in range(0, tokens, 64):
                        mutual += products[pair][row : row + 64, lanes] * weights[row : row + 64, :]
                    out[pair, 4:5, start : start + LANES] = jnp.sum(mutual, axis=0, keepdims=True)


def mutual(meta, products, rows, columns, others):
    pairs = len(products)
    tokens = products[0].shape[0]
    shape = jax.ShapeDtypeStruct((pairs, 8, tokens // 2), jnp.float32)
    return pl.pallas_call(
        functools.partial(mutual_kernel, pairs),
        in_specs=[SMEM] + [VMEM] * (2 * pairs + 2),
        out_specs=[VMEM] * 2,
        out_shape=[shape] * 2,
        scratch_shapes=[pltpu.VMEM((tokens, LANES), jnp.float32)],
        compiler_params=pltpu.CompilerParams(vmem_limit_bytes=20 * 1024 * 1024),
    )(meta, *products, *rows, columns, others)


def shards(picture_descriptors, image_slot, group_images, pair_target, pair_count):
    chips = lax.axis_size("chip")
    cores = lax.axis_size("core")
    quads = lax.axis_size("quad")
    groups = chips * cores
    chip = lax.axis_index("chip").astype(jnp.int32)
    core = lax.axis_index("core").astype(jnp.int32)
    quad = lax.axis_index("quad").astype(jnp.int32)
    images_dev, slab, width = picture_descriptors.shape
    pairs = pair_target.shape[0]
    chip_rows = images_dev * cores
    image_rows = slab * quads // IMG_W
    multiplier = 1.0 / (width * SHARPNESS_DIVISOR)

    def all_pairs(array):
        return lax.all_to_all(array, ("chip", "core"), split_axis=0, concat_axis=0, tiled=True)

    traded = lax.ppermute(picture_descriptors, "core", [(i, (i + 1) % cores) for i in range(cores)])

    asked = all_pairs(announce(groups, image_slot, group_images, pair_target, pair_count))

    capacities = [size for size in CAPACITIES if size < chip_rows] + [chip_rows]
    index, listed, branch = plan(chip_rows, 2 * pairs, capacities, chip[None], asked.reshape(groups, LANES))
    halves = (images_dev, cores, chips, slab // groups, width)

    def exchange(capacity, operands):
        own, other, rows, index = operands
        pieces = pick(capacity, core[None], rows, own, other)
        spread = lax.all_to_all(pieces, "chip", split_axis=0, concat_axis=0, tiled=True)
        return regroup(groups, 2 * pairs, index, spread)

    pieces = lax.switch(
        branch[0],
        [functools.partial(exchange, size) for size in capacities],
        (picture_descriptors.reshape(halves), traded.reshape(halves), listed, index),
    )
    maps = all_pairs(pieces).reshape(chips, cores, *pieces.shape[1:])

    def trade(array, flip):
        return lax.ppermute(array, "quad", [(i, i ^ flip) for i in range(quads)])

    query_flip, target_flip = 1, quads - 1
    meta = jnp.stack([quad, pair_count[0], quad, quad ^ target_flip])
    products, rows, columns = [], [], ()
    for pair in range(pairs):
        near_query = trade(maps[:, :, pair : pair + 1], query_flip)
        near_target = trade(maps[:, :, pairs + pair : pairs + pair + 1], target_flip)
        product, row, column = score(image_rows, multiplier, pair, meta, maps, near_query, near_target, columns)
        products.append(product)
        rows.append(row)
        columns = (column,)
    kept, sent = mutual(meta, products, rows, columns[0], trade(columns[0], target_flip))
    partial = jnp.stack([kept, trade(sent, query_flip)])
    top = partial[:, :, 0]
    weight = jnp.exp(top - jnp.max(top, axis=0, keepdims=True))
    total = jnp.sum(partial[:, :, 1] * weight, axis=0)
    fields = [jnp.sum(partial[:, :, 2 + field] * weight, axis=0) / total for field in range(3)]
    in_use = jnp.arange(pairs, dtype=jnp.int32) < pair_count[0]
    return jnp.where(in_use[None, :, None], jnp.stack(fields), 0.0).transpose(1, 0, 2)


def solution(mesh):
    pair_axis = ("chip", "core")
    split = Mesh(mesh.devices.reshape(-1, CORES, mesh.devices.shape[-1]), (*pair_axis, "quad"))
    return jax.shard_map(
        shards,
        mesh=split,
        in_specs=(P(pair_axis, "quad", None), P(), P(pair_axis), P(pair_axis), P(pair_axis)),
        out_specs=P(pair_axis, None, "quad"),
        check_vma=False,
    )
```

```python
import functools

import jax
import jax.numpy as jnp
from jax import lax
from jax.experimental import pallas as pl
from jax.experimental.pallas import tpu as pltpu
from jax.sharding import Mesh
from jax.sharding import PartitionSpec as P

IMG_W = 64
TGT_G = 8
SHARPNESS_DIVISOR = 0.1
LANES = 128
CORES = 2
PLACE_BITS = 6
PLACES = 1 << PLACE_BITS
CAPACITIES = (6, 7, 8, 9, 10, 11, 12, 16)
ANY = pl.BlockSpec(memory_space=pl.ANY)
SMEM = pl.BlockSpec(memory_space=pltpu.SMEM)
VMEM = pl.BlockSpec(memory_space=pltpu.VMEM)


def announce_kernel(pairs, image_slot, group_images, pair_target, pair_count, out):
    lane = lax.broadcasted_iota(jnp.int32, out.shape, 2)
    message = jnp.full(out.shape, -1, jnp.int32)
    for entry in range(2 * pairs):
        pair = entry % pairs
        member = TGT_G + pair if entry < pairs else pair_target[pair]
        stored = jnp.where(pair < pair_count[0], image_slot[group_images[member]], -1)
        message = jnp.where(lane == entry, stored, message)
    out[...] = message


def announce(groups, image_slot, group_images, pair_target, pair_count):
    return pl.pallas_call(
        functools.partial(announce_kernel, pair_target.shape[0]),
        in_specs=[SMEM] * 4,
        out_specs=VMEM,
        out_shape=jax.ShapeDtypeStruct((groups, 1, LANES), jnp.int32),
    )(image_slot, group_images, pair_target, pair_count)


def plan_kernel(chip_rows, entries, capacities, chip, asked, index, rows, branch):
    groups = asked.shape[0]
    table = asked[...].T
    chips_of, rows_of, stored_of = [], [], []
    wide = lax.broadcasted_iota(jnp.int32, (chip_rows, groups), 0)
    count = jnp.zeros((chip_rows, chip_rows), jnp.float32)
    for entry in range(entries):
        stored = table[entry : entry + 1, :]
        valid = jnp.where(stored >= 0, 1.0, 0.0)
        stored_of.append(jnp.maximum(stored, 0))
        chips_of.append(jnp.where(lax.div(stored_of[-1], chip_rows) == wide, valid, 0.0))
        rows_of.append(jnp.where(lax.rem(stored_of[-1], chip_rows) == wide, 1.0, 0.0))
        count += lax.dot_general(
            rows_of[-1], chips_of[-1], (((1,), (1,)), ((), ())), preferred_element_type=jnp.float32
        )
    flags = jnp.where(count > 0.0, 1.0, 0.0)
    first = lax.broadcasted_iota(jnp.int32, (chip_rows, chip_rows), 0)
    second = lax.broadcasted_iota(jnp.int32, (chip_rows, chip_rows), 1)
    earlier = jnp.dot(jnp.where(second < first, 1.0, 0.0), flags, preferred_element_type=jnp.float32)
    most = jnp.max(earlier + flags)
    choice = jnp.int32(0)
    for capacity in capacities[:-1]:
        choice += jnp.where(most > capacity, 1, 0)
    branch[0] = choice

    here = second == chip[0]
    my_flag = jnp.max(jnp.where(here, flags, 0.0), axis=1, keepdims=True)
    my_place = jnp.max(jnp.where(here, earlier, 0.0), axis=1, keepdims=True)
    slot = lax.broadcasted_iota(jnp.int32, (chip_rows, LANES), 1).astype(jnp.float32)
    row = lax.broadcasted_iota(jnp.int32, (chip_rows, LANES), 0).astype(jnp.float32)
    chosen = jnp.where((my_flag > 0.0) & (my_place == slot), row, 0.0)
    rows[...] = jnp.broadcast_to(jnp.sum(chosen, axis=0, keepdims=True), rows.shape).astype(jnp.int32)

    for entry in range(entries):
        places = jnp.dot(earlier, chips_of[entry], preferred_element_type=jnp.float32) * rows_of[entry]
        place = jnp.sum(places, axis=0, keepdims=True).astype(jnp.int32)
        index[entry : entry + 1, :] = lax.div(stored_of[entry], chip_rows) * PLACES + place


def plan(chip_rows, entries, capacities, chip, asked):
    groups = asked.shape[0]
    return pl.pallas_call(
        functools.partial(plan_kernel, chip_rows, entries, capacities),
        in_specs=[SMEM, VMEM],
        out_specs=(VMEM, VMEM, SMEM),
        out_shape=(
            jax.ShapeDtypeStruct((8, groups), jnp.int32),
            jax.ShapeDtypeStruct((8, LANES), jnp.int32),
            jax.ShapeDtypeStruct((1,), jnp.int32),
        ),
    )(chip, asked)


def pick_kernel(core, rows, own, other, out, sems):
    images_dev = own.shape[0]
    capacity = out.shape[1]
    for slot in range(capacity):
        row = rows[0, slot]
        local = lax.rem(row, images_dev)
        is_own = lax.div(row, images_dev) == core[0]

        @pl.when(is_own)
        def _():
            pltpu.make_async_copy(own.at[local, core[0]], out.at[:, slot], sems.at[slot]).start()

        @pl.when(jnp.logical_not(is_own))
        def _():
            pltpu.make_async_copy(other.at[local, core[0]], out.at[:, slot], sems.at[slot]).start()

    for slot in range(capacity):
        pltpu.make_async_copy(other.at[0, 0], out.at[:, slot], sems.at[slot]).wait()


def pick(capacity, core, rows, own, other):
    _, _, chips, piece, width = other.shape
    return pl.pallas_call(
        pick_kernel,
        in_specs=[SMEM, SMEM, ANY, ANY],
        out_specs=VMEM,
        out_shape=jax.ShapeDtypeStruct((chips, capacity, piece, width), other.dtype),
        scratch_shapes=[pltpu.SemaphoreType.DMA((capacity,))],
        compiler_params=pltpu.CompilerParams(vmem_limit_bytes=24 * 1024 * 1024),
    )(core, rows, own, other)


def regroup_kernel(index, spread, out):
    groups, entries = out.shape[:2]

    def step(group, carry):
        for entry in range(entries):
            code = index[entry, group]
            out[group, entry] = spread[code >> PLACE_BITS, code & (PLACES - 1)]
        return carry

    lax.fori_loop(0, groups, step, 0, unroll=8)


def regroup(groups, entries, index, spread):
    return pl.pallas_call(
        regroup_kernel,
        in_specs=[SMEM, VMEM],
        out_specs=VMEM,
        out_shape=jax.ShapeDtypeStruct((groups, entries, *spread.shape[2:]), spread.dtype),
        compiler_params=pltpu.CompilerParams(vmem_limit_bytes=24 * 1024 * 1024),
    )(index, spread)


def columns_kernel(multiplier, pair, meta, maps, near_query, near_target, *refs):
    *earlier, scores, powers, columns, stats = refs
    for previous in earlier:
        columns[0:pair] = previous[...]
    chips, cores, entries, piece, width = maps.shape
    part = chips * piece
    slab = cores * part
    targets = ((maps, entries // 2 + pair), (near_target, 0))
    queries = ((maps, pair), (near_query, 0))

    @pl.when(pair < meta[1])
    def _():
        for row in range(2 * cores):
            target, entry = targets[row // cores]
            tokens = target[:, row % cores, entry].reshape(part, width)
            for column in range(2 * cores):
                query, entry = queries[column // cores]
                scores[row * part : (row + 1) * part, column * part : (column + 1) * part] = (
                    lax.dot_general(
                        tokens, query[:, column % cores, entry].reshape(part, width), (((1,), (1,)), ((), ())),
                        preferred_element_type=jnp.float32,
                    )
                    * multiplier
                )

        first_lane = lax.broadcasted_iota(jnp.int32, (64, LANES), 1) == 0
        for start in range(0, 2 * slab, 64):
            block = slice(start, start + 64)
            top = jnp.max(scores[block, :], axis=1, keepdims=True)
            exponentials = jnp.exp(scores[block, :] - top)
            powers[block, :] = exponentials
            stats[block, :] = jnp.where(first_lane, top, jnp.sum(exponentials, axis=1, keepdims=True))
        for start in range(0, 2 * slab, LANES):
            columns[pair, :, start : start + LANES] = stats[start : start + LANES, :].T[0:8, :]


def score_columns(multiplier, pair, meta, maps, near_query, near_target, earlier):
    chips, cores, _, piece, width = maps.shape
    tokens = 2 * chips * cores * piece
    square = jax.ShapeDtypeStruct((tokens, tokens), jnp.float32)
    return pl.pallas_call(
        functools.partial(columns_kernel, multiplier, pair),
        in_specs=[SMEM] + [VMEM] * (3 + len(earlier)),
        out_specs=[VMEM] * 3,
        out_shape=[square, square, jax.ShapeDtypeStruct((pair + 1, 8, tokens), jnp.float32)],
        scratch_shapes=[pltpu.VMEM((tokens, LANES), jnp.float32)],
        compiler_params=pltpu.CompilerParams(vmem_limit_bytes=16 * 1024 * 1024),
        cost_estimate=pl.CostEstimate(
            flops=2 * tokens * tokens * width, bytes_accessed=2 << 20, transcendentals=1 << 20
        ),
    )(meta, maps, near_query, near_target, *earlier)


def rows_kernel(image_rows, pair, meta, scores, powers, products, rows):
    tokens = scores.shape[0]
    bands = tokens // (2 * IMG_W)

    @pl.when(pair < meta[1])
    def _():
        along = lax.broadcasted_iota(jnp.int32, (IMG_W, LANES), 0).astype(jnp.float32)
        coord_x = (2.0 * along + 1.0) / IMG_W - 1.0
        for start in range(0, tokens, LANES):
            lanes = slice(start, start + LANES)
            top = jnp.max(scores[:, lanes], axis=0, keepdims=True)
            total = jnp.zeros((8, LANES), jnp.float32)
            weighted_y = jnp.zeros((8, LANES), jnp.float32)
            folded = jnp.zeros((IMG_W, LANES), jnp.float32)
            for band in range(2 * bands):
                block = slice(band * IMG_W, (band + 1) * IMG_W)
                exponentials = jnp.exp(scores[block, lanes] - top)
                products[block, lanes] = powers[block, lanes] * exponentials
                folded += exponentials
                sums = jnp.sum(exponentials.reshape(IMG_W // 8, 8, LANES), axis=0)
                total += sums
                image_row = meta[2 + band // bands] * bands + band % bands
                weighted_y += sums * ((2.0 * image_row.astype(jnp.float32) + 1.0) / image_rows - 1.0)
            rows[0:1, lanes] = top
            rows[1:2, lanes] = jnp.sum(total, axis=0, keepdims=True)
            rows[2:3, lanes] = jnp.sum(folded * coord_x, axis=0, keepdims=True)
            rows[3:4, lanes] = jnp.sum(weighted_y, axis=0, keepdims=True)


def score_rows(image_rows, pair, meta, scores, powers):
    tokens = scores.shape[0]
    return pl.pallas_call(
        functools.partial(rows_kernel, image_rows, pair),
        in_specs=[SMEM] + [VMEM] * 2,
        out_specs=[VMEM] * 2,
        out_shape=[
            jax.ShapeDtypeStruct((tokens, tokens), jnp.float32),
            jax.ShapeDtypeStruct((8, tokens), jnp.float32),
        ],
        input_output_aliases={2: 0},
        compiler_params=pltpu.CompilerParams(vmem_limit_bytes=20 * 1024 * 1024),
        cost_estimate=pl.CostEstimate(flops=10 << 20, bytes_accessed=8 << 20, transcendentals=1 << 20),
    )(meta, scores, powers)


def mutual_kernel(pairs, meta, *refs):
    products, rows = refs[:pairs], refs[pairs : 2 * pairs]
    columns, others, kept, sent, weights = refs[2 * pairs :]
    tokens = weights.shape[0]
    slab = tokens // 2
    for pair in range(pairs):

        @pl.when(pair < meta[1])
        def _():
            for start in range(0, tokens, LANES):
                here = slice(start, start + LANES)
                there = slice((start + slab) % tokens, (start + slab) % tokens + LANES)
                top = columns[pair, 0:1, here]
                other_top = others[pair, 0:1, there]
                highest = jnp.maximum(top, other_top)
                scale = jnp.exp(top - highest)
                total = columns[pair, 1:2, here] * scale + others[pair, 1:2, there] * jnp.exp(other_top - highest)
                weights[here, :] = jnp.broadcast_to(scale / total, (LANES, LANES)).T

            for half, out in enumerate((kept, sent)):
                out[pair, 0:4, :] = rows[pair][0:4, half * slab : (half + 1) * slab]
                for start in range(0, slab, LANES):
                    lanes = slice(half * slab + start, half * slab + start + LANES)
                    mutual = jnp.zeros((64, LANES), jnp.float32)
                    for row in range(0, tokens, 64):
                        mutual += products[pair][row : row + 64, lanes] * weights[row : row + 64, :]
                    out[pair, 4:5, start : start + LANES] = jnp.sum(mutual, axis=0, keepdims=True)


def mutual(meta, products, rows, columns, others):
    pairs = len(products)
    tokens = products[0].shape[0]
    shape = jax.ShapeDtypeStruct((pairs, 8, tokens // 2), jnp.float32)
    return pl.pallas_call(
        functools.partial(mutual_kernel, pairs),
        in_specs=[SMEM] + [VMEM] * (2 * pairs + 2),
        out_specs=[VMEM] * 2,
        out_shape=[shape] * 2,
        scratch_shapes=[pltpu.VMEM((tokens, LANES), jnp.float32)],
        compiler_params=pltpu.CompilerParams(vmem_limit_bytes=20 * 1024 * 1024),
    )(meta, *products, *rows, columns, others)


def shards(picture_descriptors, image_slot, group_images, pair_target, pair_count):
    chips = lax.axis_size("chip")
    cores = lax.axis_size("core")
    quads = lax.axis_size("quad")
    groups = chips * cores
    chip = lax.axis_index("chip").astype(jnp.int32)
    core = lax.axis_index("core").astype(jnp.int32)
    quad = lax.axis_index("quad").astype(jnp.int32)
    images_dev, slab, width = picture_descriptors.shape
    pairs = pair_target.shape[0]
    chip_rows = images_dev * cores
    image_rows = slab * quads // IMG_W
    multiplier = 1.0 / (width * SHARPNESS_DIVISOR)

    def all_pairs(array):
        return lax.all_to_all(array, ("chip", "core"), split_axis=0, concat_axis=0, tiled=True)

    traded = lax.ppermute(picture_descriptors, "core", [(i, (i + 1) % cores) for i in range(cores)])

    asked = all_pairs(announce(groups, image_slot, group_images, pair_target, pair_count))

    capacities = [size for size in CAPACITIES if size < chip_rows] + [chip_rows]
    index, listed, branch = plan(chip_rows, 2 * pairs, capacities, chip[None], asked.reshape(groups, LANES))
    halves = (images_dev, cores, chips, slab // groups, width)

    def exchange(capacity, operands):
        own, other, rows, index = operands
        pieces = pick(capacity, core[None], rows, own, other)
        spread = lax.all_to_all(pieces, "chip", split_axis=0, concat_axis=0, tiled=True)
        return regroup(groups, 2 * pairs, index, spread)

    pieces = lax.switch(
        branch[0],
        [functools.partial(exchange, size) for size in capacities],
        (picture_descriptors.reshape(halves), traded.reshape(halves), listed, index),
    )
    maps = all_pairs(pieces).reshape(chips, cores, *pieces.shape[1:])

    def trade(array, flip):
        return lax.ppermute(array, "quad", [(i, i ^ flip) for i in range(quads)])

    query_flip, target_flip = 1, quads - 1
    meta = jnp.stack([quad, pair_count[0], quad, quad ^ target_flip])
    columns, squares = (), []
    for pair in range(pairs):
        near_query = trade(maps[:, :, pair : pair + 1], query_flip)
        near_target = trade(maps[:, :, pairs + pair : pairs + pair + 1], target_flip)
        scores, powers, column = score_columns(multiplier, pair, meta, maps, near_query, near_target, columns)
        squares.append((scores, powers))
        columns = (column,)
    others = trade(columns[0], target_flip)
    products, rows = zip(*(score_rows(image_rows, pair, meta, *square) for pair, square in enumerate(squares)))
    kept, sent = mutual(meta, products, rows, columns[0], others)
    partial = jnp.stack([kept, trade(sent, query_flip)])
    top = partial[:, :, 0]
    weight = jnp.exp(top - jnp.max(top, axis=0, keepdims=True))
    total = jnp.sum(partial[:, :, 1] * weight, axis=0)
    fields = [jnp.sum(partial[:, :, 2 + field] * weight, axis=0) / total for field in range(3)]
    in_use = jnp.arange(pairs, dtype=jnp.int32) < pair_count[0]
    return jnp.where(in_use[None, :, None], jnp.stack(fields), 0.0).transpose(1, 0, 2)


def solution(mesh):
    pair_axis = ("chip", "core")
    split = Mesh(mesh.devices.reshape(-1, CORES, mesh.devices.shape[-1]), (*pair_axis, "quad"))
    return jax.shard_map(
        shards,
        mesh=split,
        in_specs=(P(pair_axis, "quad", None), P(), P(pair_axis), P(pair_axis), P(pair_axis)),
        out_specs=P(pair_axis, None, "quad"),
        check_vma=False,
    )
```

```python
import functools

import jax
import jax.numpy as jnp
from jax import lax
from jax.experimental import pallas as pl
from jax.experimental.pallas import tpu as pltpu
from jax.sharding import Mesh
from jax.sharding import PartitionSpec as P

IMG_W = 64
TGT_G = 8
SHARPNESS_DIVISOR = 0.1
LANES = 128
CORES = 2
PLACE_BITS = 6
PLACES = 1 << PLACE_BITS
CAPACITIES = (6, 7, 8, 9, 10, 11, 12, 16)
ANY = pl.BlockSpec(memory_space=pl.ANY)
SMEM = pl.BlockSpec(memory_space=pltpu.SMEM)
VMEM = pl.BlockSpec(memory_space=pltpu.VMEM)


def announce_kernel(pairs, image_slot, group_images, pair_target, pair_count, out):
    lane = lax.broadcasted_iota(jnp.int32, out.shape, 2)
    message = jnp.full(out.shape, -1, jnp.int32)
    for entry in range(2 * pairs):
        pair = entry % pairs
        member = TGT_G + pair if entry < pairs else pair_target[pair]
        stored = jnp.where(pair < pair_count[0], image_slot[group_images[member]], -1)
        message = jnp.where(lane == entry, stored, message)
    out[...] = message


def announce(groups, image_slot, group_images, pair_target, pair_count):
    return pl.pallas_call(
        functools.partial(announce_kernel, pair_target.shape[0]),
        in_specs=[SMEM] * 4,
        out_specs=VMEM,
        out_shape=jax.ShapeDtypeStruct((groups, 1, LANES), jnp.int32),
    )(image_slot, group_images, pair_target, pair_count)


def plan_kernel(chip_rows, entries, capacities, chip, asked, index, rows, branch):
    groups = asked.shape[0]
    table = asked[...].T
    chips_of, rows_of, stored_of = [], [], []
    wide = lax.broadcasted_iota(jnp.int32, (chip_rows, groups), 0)
    count = jnp.zeros((chip_rows, chip_rows), jnp.float32)
    for entry in range(entries):
        stored = table[entry : entry + 1, :]
        valid = jnp.where(stored >= 0, 1.0, 0.0)
        stored_of.append(jnp.maximum(stored, 0))
        chips_of.append(jnp.where(lax.div(stored_of[-1], chip_rows) == wide, valid, 0.0))
        rows_of.append(jnp.where(lax.rem(stored_of[-1], chip_rows) == wide, 1.0, 0.0))
        count += lax.dot_general(
            rows_of[-1], chips_of[-1], (((1,), (1,)), ((), ())), preferred_element_type=jnp.float32
        )
    flags = jnp.where(count > 0.0, 1.0, 0.0)
    first = lax.broadcasted_iota(jnp.int32, (chip_rows, chip_rows), 0)
    second = lax.broadcasted_iota(jnp.int32, (chip_rows, chip_rows), 1)
    earlier = jnp.dot(jnp.where(second < first, 1.0, 0.0), flags, preferred_element_type=jnp.float32)
    most = jnp.max(earlier + flags)
    choice = jnp.int32(0)
    for capacity in capacities[:-1]:
        choice += jnp.where(most > capacity, 1, 0)
    branch[0] = choice

    here = second == chip[0]
    my_flag = jnp.max(jnp.where(here, flags, 0.0), axis=1, keepdims=True)
    my_place = jnp.max(jnp.where(here, earlier, 0.0), axis=1, keepdims=True)
    slot = lax.broadcasted_iota(jnp.int32, (chip_rows, LANES), 1).astype(jnp.float32)
    row = lax.broadcasted_iota(jnp.int32, (chip_rows, LANES), 0).astype(jnp.float32)
    chosen = jnp.where((my_flag > 0.0) & (my_place == slot), row, 0.0)
    rows[...] = jnp.broadcast_to(jnp.sum(chosen, axis=0, keepdims=True), rows.shape).astype(jnp.int32)

    for entry in range(entries):
        places = jnp.dot(earlier, chips_of[entry], preferred_element_type=jnp.float32) * rows_of[entry]
        place = jnp.sum(places, axis=0, keepdims=True).astype(jnp.int32)
        index[entry : entry + 1, :] = lax.div(stored_of[entry], chip_rows) * PLACES + place


def plan(chip_rows, entries, capacities, chip, asked):
    groups = asked.shape[0]
    return pl.pallas_call(
        functools.partial(plan_kernel, chip_rows, entries, capacities),
        in_specs=[SMEM, VMEM],
        out_specs=(VMEM, VMEM, SMEM),
        out_shape=(
            jax.ShapeDtypeStruct((8, groups), jnp.int32),
            jax.ShapeDtypeStruct((8, LANES), jnp.int32),
            jax.ShapeDtypeStruct((1,), jnp.int32),
        ),
    )(chip, asked)


def pick_kernel(core, rows, own, other, out, sems):
    images_dev = own.shape[0]
    capacity = out.shape[1]
    for slot in range(capacity):
        row = rows[0, slot]
        local = lax.rem(row, images_dev)
        is_own = lax.div(row, images_dev) == core[0]

        @pl.when(is_own)
        def _():
            pltpu.make_async_copy(own.at[local, core[0]], out.at[:, slot], sems.at[slot]).start()

        @pl.when(jnp.logical_not(is_own))
        def _():
            pltpu.make_async_copy(other.at[local, core[0]], out.at[:, slot], sems.at[slot]).start()

    for slot in range(capacity):
        pltpu.make_async_copy(other.at[0, 0], out.at[:, slot], sems.at[slot]).wait()


def pick(capacity, core, rows, own, other):
    _, _, chips, piece, width = other.shape
    return pl.pallas_call(
        pick_kernel,
        in_specs=[SMEM, SMEM, ANY, ANY],
        out_specs=VMEM,
        out_shape=jax.ShapeDtypeStruct((chips, capacity, piece, width), other.dtype),
        scratch_shapes=[pltpu.SemaphoreType.DMA((capacity,))],
        compiler_params=pltpu.CompilerParams(vmem_limit_bytes=24 * 1024 * 1024),
    )(core, rows, own, other)


def regroup_kernel(index, spread, out):
    groups, entries = out.shape[:2]

    def step(group, carry):
        for entry in range(entries):
            code = index[entry, group]
            out[group, entry] = spread[code >> PLACE_BITS, code & (PLACES - 1)]
        return carry

    lax.fori_loop(0, groups, step, 0, unroll=8)


def regroup(groups, entries, index, spread):
    return pl.pallas_call(
        regroup_kernel,
        in_specs=[SMEM, VMEM],
        out_specs=VMEM,
        out_shape=jax.ShapeDtypeStruct((groups, entries, *spread.shape[2:]), spread.dtype),
        compiler_params=pltpu.CompilerParams(vmem_limit_bytes=24 * 1024 * 1024),
    )(index, spread)


def columns_kernel(multiplier, pair, meta, maps, near_query, near_target, *refs):
    *earlier, scores, powers, columns, stats = refs
    for previous in earlier:
        columns[0:pair] = previous[...]
    chips, cores, entries, piece, width = maps.shape
    part = chips * piece
    slab = cores * part
    targets = ((maps, entries // 2 + pair), (near_target, 0))
    queries = ((maps, pair), (near_query, 0))

    @pl.when(pair < meta[1])
    def _():
        for row in range(2 * cores):
            target, entry = targets[row // cores]
            tokens = target[:, row % cores, entry].reshape(part, width)
            for column in range(2 * cores):
                query, entry = queries[column // cores]
                scores[row * part : (row + 1) * part, column * part : (column + 1) * part] = (
                    lax.dot_general(
                        tokens, query[:, column % cores, entry].reshape(part, width), (((1,), (1,)), ((), ())),
                        preferred_element_type=jnp.float32,
                    )
                    * multiplier
                )

        first_lane = lax.broadcasted_iota(jnp.int32, (64, LANES), 1) == 0
        for start in range(0, 2 * slab, 64):
            block = slice(start, start + 64)
            top = jnp.max(scores[block, :], axis=1, keepdims=True)
            exponentials = jnp.exp(scores[block, :] - top)
            powers[block, :] = exponentials
            stats[block, :] = jnp.where(first_lane, top, jnp.sum(exponentials, axis=1, keepdims=True))
        for start in range(0, 2 * slab, LANES):
            columns[pair, :, start : start + LANES] = stats[start : start + LANES, :].T[0:8, :]


def score_columns(multiplier, pair, meta, maps, near_query, near_target, earlier):
    chips, cores, _, piece, width = maps.shape
    tokens = 2 * chips * cores * piece
    square = jax.ShapeDtypeStruct((tokens, tokens), jnp.float32)
    return pl.pallas_call(
        functools.partial(columns_kernel, multiplier, pair),
        in_specs=[SMEM] + [VMEM] * (3 + len(earlier)),
        out_specs=[VMEM] * 3,
        out_shape=[square, square, jax.ShapeDtypeStruct((pair + 1, 8, tokens), jnp.float32)],
        scratch_shapes=[pltpu.VMEM((tokens, LANES), jnp.float32)],
        compiler_params=pltpu.CompilerParams(vmem_limit_bytes=16 * 1024 * 1024),
        cost_estimate=pl.CostEstimate(
            flops=2 * tokens * tokens * width, bytes_accessed=2 << 20, transcendentals=1 << 20
        ),
    )(meta, maps, near_query, near_target, *earlier)


def rows_kernel(image_rows, pair, meta, scores, powers, products, rows):
    tokens = scores.shape[0]
    bands = tokens // (2 * IMG_W)

    @pl.when(pair < meta[1])
    def _():
        along = lax.broadcasted_iota(jnp.int32, (IMG_W, LANES), 0).astype(jnp.float32)
        coord_x = (2.0 * along + 1.0) / IMG_W - 1.0
        for start in range(0, tokens, LANES):
            lanes = slice(start, start + LANES)
            top = jnp.max(scores[:, lanes], axis=0, keepdims=True)
            total = jnp.zeros((8, LANES), jnp.float32)
            weighted_y = jnp.zeros((8, LANES), jnp.float32)
            folded = jnp.zeros((IMG_W, LANES), jnp.float32)
            for band in range(2 * bands):
                block = slice(band * IMG_W, (band + 1) * IMG_W)
                exponentials = jnp.exp(scores[block, lanes] - top)
                products[block, lanes] = powers[block, lanes] * exponentials
                folded += exponentials
                sums = jnp.sum(exponentials.reshape(IMG_W // 8, 8, LANES), axis=0)
                total += sums
                image_row = meta[2 + band // bands] * bands + band % bands
                weighted_y += sums * ((2.0 * image_row.astype(jnp.float32) + 1.0) / image_rows - 1.0)
            rows[0:1, lanes] = top
            rows[1:2, lanes] = jnp.sum(total, axis=0, keepdims=True)
            rows[2:3, lanes] = jnp.sum(folded * coord_x, axis=0, keepdims=True)
            rows[3:4, lanes] = jnp.sum(weighted_y, axis=0, keepdims=True)


def score_rows(image_rows, pair, meta, scores, powers):
    tokens = scores.shape[0]
    return pl.pallas_call(
        functools.partial(rows_kernel, image_rows, pair),
        in_specs=[SMEM] + [VMEM] * 2,
        out_specs=[VMEM] * 2,
        out_shape=[
            jax.ShapeDtypeStruct((tokens, tokens), jnp.float32),
            jax.ShapeDtypeStruct((8, tokens), jnp.float32),
        ],
        compiler_params=pltpu.CompilerParams(vmem_limit_bytes=16 * 1024 * 1024),
        cost_estimate=pl.CostEstimate(flops=10 << 20, bytes_accessed=8 << 20, transcendentals=1 << 20),
    )(meta, scores, powers)


def mutual_kernel(pairs, meta, *refs):
    products, rows = refs[:pairs], refs[pairs : 2 * pairs]
    columns, others, kept, sent, weights = refs[2 * pairs :]
    tokens = weights.shape[0]
    slab = tokens // 2
    for pair in range(pairs):

        @pl.when(pair < meta[1])
        def _():
            for start in range(0, tokens, LANES):
                here = slice(start, start + LANES)
                there = slice((start + slab) % tokens, (start + slab) % tokens + LANES)
                top = columns[pair, 0:1, here]
                other_top = others[pair, 0:1, there]
                highest = jnp.maximum(top, other_top)
                scale = jnp.exp(top - highest)
                total = columns[pair, 1:2, here] * scale + others[pair, 1:2, there] * jnp.exp(other_top - highest)
                weights[here, :] = jnp.broadcast_to(scale / total, (LANES, LANES)).T

            for half, out in enumerate((kept, sent)):
                out[pair, 0:4, :] = rows[pair][0:4, half * slab : (half + 1) * slab]
                for start in range(0, slab, LANES):
                    lanes = slice(half * slab + start, half * slab + start + LANES)
                    mutual = jnp.zeros((64, LANES), jnp.float32)
                    for row in range(0, tokens, 64):
                        mutual += products[pair][row : row + 64, lanes] * weights[row : row + 64, :]
                    out[pair, 4:5, start : start + LANES] = jnp.sum(mutual, axis=0, keepdims=True)


def mutual(meta, products, rows, columns, others):
    pairs = len(products)
    tokens = products[0].shape[0]
    shape = jax.ShapeDtypeStruct((pairs, 8, tokens // 2), jnp.float32)
    return pl.pallas_call(
        functools.partial(mutual_kernel, pairs),
        in_specs=[SMEM] + [VMEM] * (2 * pairs + 2),
        out_specs=[VMEM] * 2,
        out_shape=[shape] * 2,
        scratch_shapes=[pltpu.VMEM((tokens, LANES), jnp.float32)],
        compiler_params=pltpu.CompilerParams(vmem_limit_bytes=20 * 1024 * 1024),
    )(meta, *products, *rows, columns, others)


def shards(picture_descriptors, image_slot, group_images, pair_target, pair_count):
    chips = lax.axis_size("chip")
    cores = lax.axis_size("core")
    quads = lax.axis_size("quad")
    groups = chips * cores
    chip = lax.axis_index("chip").astype(jnp.int32)
    core = lax.axis_index("core").astype(jnp.int32)
    quad = lax.axis_index("quad").astype(jnp.int32)
    images_dev, slab, width = picture_descriptors.shape
    pairs = pair_target.shape[0]
    chip_rows = images_dev * cores
    image_rows = slab * quads // IMG_W
    multiplier = 1.0 / (width * SHARPNESS_DIVISOR)

    def all_pairs(array):
        return lax.all_to_all(array, ("chip", "core"), split_axis=0, concat_axis=0, tiled=True)

    traded = lax.ppermute(picture_descriptors, "core", [(i, (i + 1) % cores) for i in range(cores)])

    asked = all_pairs(announce(groups, image_slot, group_images, pair_target, pair_count))

    capacities = [size for size in CAPACITIES if size < chip_rows] + [chip_rows]
    index, listed, branch = plan(chip_rows, 2 * pairs, capacities, chip[None], asked.reshape(groups, LANES))
    halves = (images_dev, cores, chips, slab // groups, width)

    def exchange(capacity, operands):
        own, other, rows, index = operands
        pieces = pick(capacity, core[None], rows, own, other)
        spread = lax.all_to_all(pieces, "chip", split_axis=0, concat_axis=0, tiled=True)
        return regroup(groups, 2 * pairs, index, spread)

    pieces = lax.switch(
        branch[0],
        [functools.partial(exchange, size) for size in capacities],
        (picture_descriptors.reshape(halves), traded.reshape(halves), listed, index),
    )
    maps = all_pairs(pieces).reshape(chips, cores, *pieces.shape[1:])

    def trade(array, flip):
        return lax.ppermute(array, "quad", [(i, i ^ flip) for i in range(quads)])

    query_flip, target_flip = 1, quads - 1
    meta = jnp.stack([quad, pair_count[0], quad, quad ^ target_flip])
    columns, squares = (), []
    for pair in range(pairs):
        near_query = trade(maps[:, :, pair : pair + 1], query_flip)
        near_target = trade(maps[:, :, pairs + pair : pairs + pair + 1], target_flip)
        scores, powers, column = score_columns(multiplier, pair, meta, maps, near_query, near_target, columns)
        squares.append((scores, powers))
        columns = (column,)
    others = trade(columns[0], target_flip)
    products, rows = zip(*(score_rows(image_rows, pair, meta, *square) for pair, square in enumerate(squares)))
    kept, sent = mutual(meta, products, rows, columns[0], others)
    partial = jnp.stack([kept, trade(sent, query_flip)])
    top = partial[:, :, 0]
    weight = jnp.exp(top - jnp.max(top, axis=0, keepdims=True))
    total = jnp.sum(partial[:, :, 1] * weight, axis=0)
    fields = [jnp.sum(partial[:, :, 2 + field] * weight, axis=0) / total for field in range(3)]
    in_use = jnp.arange(pairs, dtype=jnp.int32) < pair_count[0]
    return jnp.where(in_use[None, :, None], jnp.stack(fields), 0.0).transpose(1, 0, 2)


def solution(mesh):
    pair_axis = ("chip", "core")
    split = Mesh(mesh.devices.reshape(-1, CORES, mesh.devices.shape[-1]), (*pair_axis, "quad"))
    return jax.shard_map(
        shards,
        mesh=split,
        in_specs=(P(pair_axis, "quad", None), P(), P(pair_axis), P(pair_axis), P(pair_axis)),
        out_specs=P(pair_axis, None, "quad"),
        check_vma=False,
    )
```

```python
import functools

import jax
import jax.numpy as jnp
from jax import lax
from jax.experimental import pallas as pl
from jax.experimental.pallas import tpu as pltpu
from jax.sharding import Mesh
from jax.sharding import PartitionSpec as P

IMG_W = 64
TGT_G = 8
SHARPNESS_DIVISOR = 0.1
LANES = 128
CORES = 2
PLACE_BITS = 6
PLACES = 1 << PLACE_BITS
CAPACITIES = (6, 7, 8, 9, 10, 11, 12, 16)
ANY = pl.BlockSpec(memory_space=pl.ANY)
SMEM = pl.BlockSpec(memory_space=pltpu.SMEM)
VMEM = pl.BlockSpec(memory_space=pltpu.VMEM)


def announce_kernel(pairs, image_slot, group_images, pair_target, pair_count, out):
    lane = lax.broadcasted_iota(jnp.int32, out.shape, 2)
    message = jnp.full(out.shape, -1, jnp.int32)
    for entry in range(2 * pairs):
        pair = entry % pairs
        member = TGT_G + pair if entry < pairs else pair_target[pair]
        stored = jnp.where(pair < pair_count[0], image_slot[group_images[member]], -1)
        message = jnp.where(lane == entry, stored, message)
    out[...] = message


def announce(groups, image_slot, group_images, pair_target, pair_count):
    return pl.pallas_call(
        functools.partial(announce_kernel, pair_target.shape[0]),
        in_specs=[SMEM] * 4,
        out_specs=VMEM,
        out_shape=jax.ShapeDtypeStruct((groups, 1, LANES), jnp.int32),
    )(image_slot, group_images, pair_target, pair_count)


def plan_kernel(chip_rows, entries, capacities, chip, asked, index, rows, branch):
    groups = asked.shape[0]
    table = asked[...].T
    chips_of, rows_of, stored_of = [], [], []
    wide = lax.broadcasted_iota(jnp.int32, (chip_rows, groups), 0)
    count = jnp.zeros((chip_rows, chip_rows), jnp.float32)
    for entry in range(entries):
        stored = table[entry : entry + 1, :]
        valid = jnp.where(stored >= 0, 1.0, 0.0)
        stored_of.append(jnp.maximum(stored, 0))
        chips_of.append(jnp.where(lax.div(stored_of[-1], chip_rows) == wide, valid, 0.0))
        rows_of.append(jnp.where(lax.rem(stored_of[-1], chip_rows) == wide, 1.0, 0.0))
        count += lax.dot_general(
            rows_of[-1], chips_of[-1], (((1,), (1,)), ((), ())), preferred_element_type=jnp.float32
        )
    flags = jnp.where(count > 0.0, 1.0, 0.0)
    first = lax.broadcasted_iota(jnp.int32, (chip_rows, chip_rows), 0)
    second = lax.broadcasted_iota(jnp.int32, (chip_rows, chip_rows), 1)
    earlier = jnp.dot(jnp.where(second < first, 1.0, 0.0), flags, preferred_element_type=jnp.float32)
    most = jnp.max(earlier + flags)
    choice = jnp.int32(0)
    for capacity in capacities[:-1]:
        choice += jnp.where(most > capacity, 1, 0)
    branch[0] = choice

    here = second == chip[0]
    my_flag = jnp.max(jnp.where(here, flags, 0.0), axis=1, keepdims=True)
    my_place = jnp.max(jnp.where(here, earlier, 0.0), axis=1, keepdims=True)
    slot = lax.broadcasted_iota(jnp.int32, (chip_rows, LANES), 1).astype(jnp.float32)
    row = lax.broadcasted_iota(jnp.int32, (chip_rows, LANES), 0).astype(jnp.float32)
    chosen = jnp.where((my_flag > 0.0) & (my_place == slot), row, 0.0)
    rows[...] = jnp.broadcast_to(jnp.sum(chosen, axis=0, keepdims=True), rows.shape).astype(jnp.int32)

    for entry in range(entries):
        places = jnp.dot(earlier, chips_of[entry], preferred_element_type=jnp.float32) * rows_of[entry]
        place = jnp.sum(places, axis=0, keepdims=True).astype(jnp.int32)
        index[entry : entry + 1, :] = lax.div(stored_of[entry], chip_rows) * PLACES + place


def plan(chip_rows, entries, capacities, chip, asked):
    groups = asked.shape[0]
    return pl.pallas_call(
        functools.partial(plan_kernel, chip_rows, entries, capacities),
        in_specs=[SMEM, VMEM],
        out_specs=(VMEM, VMEM, SMEM),
        out_shape=(
            jax.ShapeDtypeStruct((8, groups), jnp.int32),
            jax.ShapeDtypeStruct((8, LANES), jnp.int32),
            jax.ShapeDtypeStruct((1,), jnp.int32),
        ),
    )(chip, asked)


def pick_kernel(core, rows, own, other, out, sems):
    images_dev = own.shape[0]
    capacity = out.shape[1]
    for slot in range(capacity):
        row = rows[0, slot]
        local = lax.rem(row, images_dev)
        is_own = lax.div(row, images_dev) == core[0]

        @pl.when(is_own)
        def _():
            pltpu.make_async_copy(own.at[local, core[0]], out.at[:, slot], sems.at[slot]).start()

        @pl.when(jnp.logical_not(is_own))
        def _():
            pltpu.make_async_copy(other.at[local, core[0]], out.at[:, slot], sems.at[slot]).start()

    for slot in range(capacity):
        pltpu.make_async_copy(other.at[0, 0], out.at[:, slot], sems.at[slot]).wait()


def pick(capacity, core, rows, own, other):
    _, _, chips, piece, width = other.shape
    return pl.pallas_call(
        pick_kernel,
        in_specs=[SMEM, SMEM, ANY, ANY],
        out_specs=VMEM,
        out_shape=jax.ShapeDtypeStruct((chips, capacity, piece, width), other.dtype),
        scratch_shapes=[pltpu.SemaphoreType.DMA((capacity,))],
        compiler_params=pltpu.CompilerParams(vmem_limit_bytes=24 * 1024 * 1024),
    )(core, rows, own, other)


def regroup_kernel(index, spread, out):
    groups, entries = out.shape[:2]

    def step(group, carry):
        for entry in range(entries):
            code = index[entry, group]
            out[group, entry] = spread[code >> PLACE_BITS, code & (PLACES - 1)]
        return carry

    lax.fori_loop(0, groups, step, 0, unroll=8)


def regroup(groups, entries, index, spread):
    return pl.pallas_call(
        regroup_kernel,
        in_specs=[SMEM, VMEM],
        out_specs=VMEM,
        out_shape=jax.ShapeDtypeStruct((groups, entries, *spread.shape[2:]), spread.dtype),
        compiler_params=pltpu.CompilerParams(vmem_limit_bytes=24 * 1024 * 1024),
    )(index, spread)


def score_kernel(image_rows, multiplier, pair, meta, maps, near_query, near_target, *refs):
    *earlier, products, rows, columns, scores, stats = refs
    for previous in earlier:
        columns[0:pair] = previous[...]
    chips, cores, entries, piece, width = maps.shape
    part = chips * piece
    slab = cores * part
    targets = ((maps, entries // 2 + pair), (near_target, 0))
    queries = ((maps, pair), (near_query, 0))

    @pl.when(pair < meta[1])
    def _():
        for row in range(2 * cores):
            target, entry = targets[row // cores]
            tokens = target[:, row % cores, entry].reshape(part, width)
            for column in range(2 * cores):
                query, entry = queries[column // cores]
                scores[row * part : (row + 1) * part, column * part : (column + 1) * part] = (
                    lax.dot_general(
                        tokens, query[:, column % cores, entry].reshape(part, width), (((1,), (1,)), ((), ())),
                        preferred_element_type=jnp.float32,
                    )
                    * multiplier
                )

        first_lane = lax.broadcasted_iota(jnp.int32, (64, LANES), 1) == 0

        def rows_step(index, carry):
            block = pl.ds(pl.multiple_of(index * 64, 64), 64)
            top = jnp.max(scores[block, :], axis=1, keepdims=True)
            powers = jnp.exp(scores[block, :] - top)
            products[block, :] = powers
            stats[block, :] = jnp.where(first_lane, top, jnp.sum(powers, axis=1, keepdims=True))
            return carry

        lax.fori_loop(0, 2 * slab // 64, rows_step, 0, unroll=16)
        for start in range(0, 2 * slab, LANES):
            columns[pair, :, start : start + LANES] = stats[start : start + LANES, :].T[0:8, :]

        bands = slab // IMG_W
        along = lax.broadcasted_iota(jnp.int32, (IMG_W, LANES), 0).astype(jnp.float32)
        coord_x = (2.0 * along + 1.0) / IMG_W - 1.0

        def lanes_step(index, carry):
            lanes = pl.ds(pl.multiple_of(index * LANES, LANES), LANES)
            top = jnp.max(scores[:, lanes], axis=0, keepdims=True)
            total = jnp.zeros((8, LANES), jnp.float32)
            weighted_y = jnp.zeros((8, LANES), jnp.float32)
            folded = jnp.zeros((IMG_W, LANES), jnp.float32)
            for band in range(2 * bands):
                block = slice(band * IMG_W, (band + 1) * IMG_W)
                powers = jnp.exp(scores[block, lanes] - top)
                products[block, lanes] *= powers
                folded += powers
                sums = jnp.sum(powers.reshape(IMG_W // 8, 8, LANES), axis=0)
                total += sums
                image_row = meta[2 + band // bands] * bands + band % bands
                weighted_y += sums * ((2.0 * image_row.astype(jnp.float32) + 1.0) / image_rows - 1.0)
            rows[0:1, lanes] = top
            rows[1:2, lanes] = jnp.sum(total, axis=0, keepdims=True)
            rows[2:3, lanes] = jnp.sum(folded * coord_x, axis=0, keepdims=True)
            rows[3:4, lanes] = jnp.sum(weighted_y, axis=0, keepdims=True)
            return carry

        lax.fori_loop(0, 2 * slab // LANES, lanes_step, 0, unroll=8)


def score(image_rows, multiplier, pair, meta, maps, near_query, near_target, earlier):
    chips, cores, _, piece, width = maps.shape
    tokens = 2 * chips * cores * piece
    return pl.pallas_call(
        functools.partial(score_kernel, image_rows, multiplier, pair),
        in_specs=[SMEM] + [VMEM] * (3 + len(earlier)),
        out_specs=[VMEM] * 3,
        out_shape=[
            jax.ShapeDtypeStruct((tokens, tokens), jnp.float32),
            jax.ShapeDtypeStruct((8, tokens), jnp.float32),
            jax.ShapeDtypeStruct((pair + 1, 8, tokens), jnp.float32),
        ],
        scratch_shapes=[pltpu.VMEM((tokens, tokens), jnp.float32), pltpu.VMEM((tokens, LANES), jnp.float32)],
        compiler_params=pltpu.CompilerParams(vmem_limit_bytes=20 * 1024 * 1024),
        cost_estimate=pl.CostEstimate(
            flops=2 * tokens * tokens * width, bytes_accessed=2 << 20, transcendentals=2 << 20
        ),
    )(meta, maps, near_query, near_target, *earlier)


def columns_kernel(multiplier, pair, meta, maps, near_query, near_target, *refs):
    *earlier, scores, powers, columns, stats = refs
    for previous in earlier:
        columns[0:pair] = previous[...]
    chips, cores, entries, piece, width = maps.shape
    part = chips * piece
    slab = cores * part
    targets = ((maps, entries // 2 + pair), (near_target, 0))
    queries = ((maps, pair), (near_query, 0))

    @pl.when(pair < meta[1])
    def _():
        for row in range(2 * cores):
            target, entry = targets[row // cores]
            tokens = target[:, row % cores, entry].reshape(part, width)
            for column in range(2 * cores):
                query, entry = queries[column // cores]
                scores[row * part : (row + 1) * part, column * part : (column + 1) * part] = (
                    lax.dot_general(
                        tokens, query[:, column % cores, entry].reshape(part, width), (((1,), (1,)), ((), ())),
                        preferred_element_type=jnp.float32,
                    )
                    * multiplier
                )

        first_lane = lax.broadcasted_iota(jnp.int32, (64, LANES), 1) == 0
        for start in range(0, 2 * slab, 64):
            block = slice(start, start + 64)
            top = jnp.max(scores[block, :], axis=1, keepdims=True)
            exponentials = jnp.exp(scores[block, :] - top)
            powers[block, :] = exponentials
            stats[block, :] = jnp.where(first_lane, top, jnp.sum(exponentials, axis=1, keepdims=True))
        for start in range(0, 2 * slab, LANES):
            columns[pair, :, start : start + LANES] = stats[start : start + LANES, :].T[0:8, :]


def score_columns(multiplier, pair, meta, maps, near_query, near_target, earlier):
    chips, cores, _, piece, width = maps.shape
    tokens = 2 * chips * cores * piece
    square = jax.ShapeDtypeStruct((tokens, tokens), jnp.float32)
    return pl.pallas_call(
        functools.partial(columns_kernel, multiplier, pair),
        in_specs=[SMEM] + [VMEM] * (3 + len(earlier)),
        out_specs=[VMEM] * 3,
        out_shape=[square, square, jax.ShapeDtypeStruct((pair + 1, 8, tokens), jnp.float32)],
        scratch_shapes=[pltpu.VMEM((tokens, LANES), jnp.float32)],
        compiler_params=pltpu.CompilerParams(vmem_limit_bytes=16 * 1024 * 1024),
        cost_estimate=pl.CostEstimate(
            flops=2 * tokens * tokens * width, bytes_accessed=2 << 20, transcendentals=1 << 20
        ),
    )(meta, maps, near_query, near_target, *earlier)


def rows_kernel(image_rows, pair, meta, scores, powers, products, rows):
    tokens = scores.shape[0]
    bands = tokens // (2 * IMG_W)

    @pl.when(pair < meta[1])
    def _():
        along = lax.broadcasted_iota(jnp.int32, (IMG_W, LANES), 0).astype(jnp.float32)
        coord_x = (2.0 * along + 1.0) / IMG_W - 1.0
        for start in range(0, tokens, LANES):
            lanes = slice(start, start + LANES)
            top = jnp.max(scores[:, lanes], axis=0, keepdims=True)
            total = jnp.zeros((8, LANES), jnp.float32)
            weighted_y = jnp.zeros((8, LANES), jnp.float32)
            folded = jnp.zeros((IMG_W, LANES), jnp.float32)
            for band in range(2 * bands):
                block = slice(band * IMG_W, (band + 1) * IMG_W)
                exponentials = jnp.exp(scores[block, lanes] - top)
                products[block, lanes] = powers[block, lanes] * exponentials
                folded += exponentials
                sums = jnp.sum(exponentials.reshape(IMG_W // 8, 8, LANES), axis=0)
                total += sums
                image_row = meta[2 + band // bands] * bands + band % bands
                weighted_y += sums * ((2.0 * image_row.astype(jnp.float32) + 1.0) / image_rows - 1.0)
            rows[0:1, lanes] = top
            rows[1:2, lanes] = jnp.sum(total, axis=0, keepdims=True)
            rows[2:3, lanes] = jnp.sum(folded * coord_x, axis=0, keepdims=True)
            rows[3:4, lanes] = jnp.sum(weighted_y, axis=0, keepdims=True)


def score_rows(image_rows, pair, meta, scores, powers):
    tokens = scores.shape[0]
    return pl.pallas_call(
        functools.partial(rows_kernel, image_rows, pair),
        in_specs=[SMEM] + [VMEM] * 2,
        out_specs=[VMEM] * 2,
        out_shape=[
            jax.ShapeDtypeStruct((tokens, tokens), jnp.float32),
            jax.ShapeDtypeStruct((8, tokens), jnp.float32),
        ],
        compiler_params=pltpu.CompilerParams(vmem_limit_bytes=16 * 1024 * 1024),
        cost_estimate=pl.CostEstimate(flops=10 << 20, bytes_accessed=8 << 20, transcendentals=1 << 20),
    )(meta, scores, powers)


def mutual_kernel(pairs, meta, *refs):
    products, rows = refs[:pairs], refs[pairs : 2 * pairs]
    columns, others, kept, sent, weights = refs[2 * pairs :]
    tokens = weights.shape[0]
    slab = tokens // 2
    for pair in range(pairs):

        @pl.when(pair < meta[1])
        def _():
            for start in range(0, tokens, LANES):
                here = slice(start, start + LANES)
                there = slice((start + slab) % tokens, (start + slab) % tokens + LANES)
                top = columns[pair, 0:1, here]
                other_top = others[pair, 0:1, there]
                highest = jnp.maximum(top, other_top)
                scale = jnp.exp(top - highest)
                total = columns[pair, 1:2, here] * scale + others[pair, 1:2, there] * jnp.exp(other_top - highest)
                weights[here, :] = jnp.broadcast_to(scale / total, (LANES, LANES)).T

            for half, out in enumerate((kept, sent)):
                out[pair, 0:4, :] = rows[pair][0:4, half * slab : (half + 1) * slab]
                for start in range(0, slab, LANES):
                    lanes = slice(half * slab + start, half * slab + start + LANES)
                    mutual = jnp.zeros((64, LANES), jnp.float32)
                    for row in range(0, tokens, 64):
                        mutual += products[pair][row : row + 64, lanes] * weights[row : row + 64, :]
                    out[pair, 4:5, start : start + LANES] = jnp.sum(mutual, axis=0, keepdims=True)


def mutual(meta, products, rows, columns, others):
    pairs = len(products)
    tokens = products[0].shape[0]
    shape = jax.ShapeDtypeStruct((pairs, 8, tokens // 2), jnp.float32)
    return pl.pallas_call(
        functools.partial(mutual_kernel, pairs),
        in_specs=[SMEM] + [VMEM] * (2 * pairs + 2),
        out_specs=[VMEM] * 2,
        out_shape=[shape] * 2,
        scratch_shapes=[pltpu.VMEM((tokens, LANES), jnp.float32)],
        compiler_params=pltpu.CompilerParams(vmem_limit_bytes=20 * 1024 * 1024),
    )(meta, *products, *rows, columns, others)


def shards(picture_descriptors, image_slot, group_images, pair_target, pair_count):
    chips = lax.axis_size("chip")
    cores = lax.axis_size("core")
    quads = lax.axis_size("quad")
    groups = chips * cores
    chip = lax.axis_index("chip").astype(jnp.int32)
    core = lax.axis_index("core").astype(jnp.int32)
    quad = lax.axis_index("quad").astype(jnp.int32)
    images_dev, slab, width = picture_descriptors.shape
    pairs = pair_target.shape[0]
    chip_rows = images_dev * cores
    image_rows = slab * quads // IMG_W
    multiplier = 1.0 / (width * SHARPNESS_DIVISOR)

    def all_pairs(array):
        return lax.all_to_all(array, ("chip", "core"), split_axis=0, concat_axis=0, tiled=True)

    traded = lax.ppermute(picture_descriptors, "core", [(i, (i + 1) % cores) for i in range(cores)])

    asked = all_pairs(announce(groups, image_slot, group_images, pair_target, pair_count))

    capacities = [size for size in CAPACITIES if size < chip_rows] + [chip_rows]
    index, listed, branch = plan(chip_rows, 2 * pairs, capacities, chip[None], asked.reshape(groups, LANES))
    halves = (images_dev, cores, chips, slab // groups, width)

    def exchange(capacity, operands):
        own, other, rows, index = operands
        pieces = pick(capacity, core[None], rows, own, other)
        spread = lax.all_to_all(pieces, "chip", split_axis=0, concat_axis=0, tiled=True)
        return regroup(groups, 2 * pairs, index, spread)

    pieces = lax.switch(
        branch[0],
        [functools.partial(exchange, size) for size in capacities],
        (picture_descriptors.reshape(halves), traded.reshape(halves), listed, index),
    )
    maps = all_pairs(pieces).reshape(chips, cores, *pieces.shape[1:])

    def trade(array, flip):
        return lax.ppermute(array, "quad", [(i, i ^ flip) for i in range(quads)])

    query_flip, target_flip = 1, quads - 1
    meta = jnp.stack([quad, pair_count[0], quad, quad ^ target_flip])
    products, rows, columns = [], [], ()
    for pair in range(pairs):
        near_query = trade(maps[:, :, pair : pair + 1], query_flip)
        near_target = trade(maps[:, :, pairs + pair : pairs + pair + 1], target_flip)
        if pair < pairs - 1:
            product, row, column = score(image_rows, multiplier, pair, meta, maps, near_query, near_target, columns)
        else:
            scores, powers, column = score_columns(multiplier, pair, meta, maps, near_query, near_target, columns)
            others = trade(column, target_flip)
            product, row = score_rows(image_rows, pair, meta, scores, powers)
        products.append(product)
        rows.append(row)
        columns = (column,)
    kept, sent = mutual(meta, products, rows, columns[0], others)
    partial = jnp.stack([kept, trade(sent, query_flip)])
    top = partial[:, :, 0]
    weight = jnp.exp(top - jnp.max(top, axis=0, keepdims=True))
    total = jnp.sum(partial[:, :, 1] * weight, axis=0)
    fields = [jnp.sum(partial[:, :, 2 + field] * weight, axis=0) / total for field in range(3)]
    in_use = jnp.arange(pairs, dtype=jnp.int32) < pair_count[0]
    return jnp.where(in_use[None, :, None], jnp.stack(fields), 0.0).transpose(1, 0, 2)


def solution(mesh):
    pair_axis = ("chip", "core")
    split = Mesh(mesh.devices.reshape(-1, CORES, mesh.devices.shape[-1]), (*pair_axis, "quad"))
    return jax.shard_map(
        shards,
        mesh=split,
        in_specs=(P(pair_axis, "quad", None), P(), P(pair_axis), P(pair_axis), P(pair_axis)),
        out_specs=P(pair_axis, None, "quad"),
        check_vma=False,
    )
```

```python
import functools

import jax
import jax.numpy as jnp
from jax import lax
from jax.experimental import pallas as pl
from jax.experimental.pallas import tpu as pltpu
from jax.sharding import Mesh
from jax.sharding import PartitionSpec as P

IMG_W = 64
TGT_G = 8
SHARPNESS_DIVISOR = 0.1
LANES = 128
CORES = 2
PLACE_BITS = 6
PLACES = 1 << PLACE_BITS
CAPACITIES = (6, 7, 8, 9, 10, 11, 12, 16)
ANY = pl.BlockSpec(memory_space=pl.ANY)
SMEM = pl.BlockSpec(memory_space=pltpu.SMEM)
VMEM = pl.BlockSpec(memory_space=pltpu.VMEM)


def announce_kernel(pairs, image_slot, group_images, pair_target, pair_count, out):
    lane = lax.broadcasted_iota(jnp.int32, out.shape, 2)
    message = jnp.full(out.shape, -1, jnp.int32)
    for entry in range(2 * pairs):
        pair = entry % pairs
        member = TGT_G + pair if entry < pairs else pair_target[pair]
        stored = jnp.where(pair < pair_count[0], image_slot[group_images[member]], -1)
        message = jnp.where(lane == entry, stored, message)
    out[...] = message


def announce(groups, image_slot, group_images, pair_target, pair_count):
    return pl.pallas_call(
        functools.partial(announce_kernel, pair_target.shape[0]),
        in_specs=[SMEM] * 4,
        out_specs=VMEM,
        out_shape=jax.ShapeDtypeStruct((groups, 1, LANES), jnp.int32),
    )(image_slot, group_images, pair_target, pair_count)


def plan_kernel(chip_rows, entries, capacities, chip, asked, places, rows, branch):
    groups = asked.shape[0]
    table = asked[...].T
    chips_of, rows_of, stored_of = [], [], []
    wide = lax.broadcasted_iota(jnp.int32, (chip_rows, groups), 0)
    count = jnp.zeros((chip_rows, chip_rows), jnp.float32)
    for entry in range(entries):
        stored = table[entry : entry + 1, :]
        valid = jnp.where(stored >= 0, 1.0, 0.0)
        stored_of.append(jnp.maximum(stored, 0))
        chips_of.append(jnp.where(lax.div(stored_of[-1], chip_rows) == wide, valid, 0.0))
        rows_of.append(jnp.where(lax.rem(stored_of[-1], chip_rows) == wide, 1.0, 0.0))
        count += lax.dot_general(
            rows_of[-1], chips_of[-1], (((1,), (1,)), ((), ())), preferred_element_type=jnp.float32
        )
    flags = jnp.where(count > 0.0, 1.0, 0.0)
    first = lax.broadcasted_iota(jnp.int32, (chip_rows, chip_rows), 0)
    second = lax.broadcasted_iota(jnp.int32, (chip_rows, chip_rows), 1)
    earlier = jnp.dot(jnp.where(second < first, 1.0, 0.0), flags, preferred_element_type=jnp.float32)
    most = jnp.max(earlier + flags)
    choice = jnp.int32(0)
    for capacity in capacities[:-1]:
        choice += jnp.where(most > capacity, 1, 0)
    branch[0] = choice

    here = second == chip[0]
    my_flag = jnp.max(jnp.where(here, flags, 0.0), axis=1, keepdims=True)
    my_place = jnp.max(jnp.where(here, earlier, 0.0), axis=1, keepdims=True)
    slot = lax.broadcasted_iota(jnp.int32, (chip_rows, LANES), 1).astype(jnp.float32)
    row = lax.broadcasted_iota(jnp.int32, (chip_rows, LANES), 0).astype(jnp.float32)
    chosen = jnp.where((my_flag > 0.0) & (my_place == slot), row, 0.0)
    rows[...] = jnp.broadcast_to(jnp.sum(chosen, axis=0, keepdims=True), rows.shape).astype(jnp.int32)

    places[...] = earlier


def locate_kernel(chip_rows, entries, places, asked, index):
    groups = asked.shape[0]
    table = asked[...].T
    wide = lax.broadcasted_iota(jnp.int32, (chip_rows, groups), 0)
    for entry in range(entries):
        stored = jnp.maximum(table[entry : entry + 1, :], 0)
        chip = lax.div(stored, chip_rows)
        by_chip = jnp.dot(places[...], jnp.where(chip == wide, 1.0, 0.0), preferred_element_type=jnp.float32)
        place = jnp.sum(jnp.where(lax.rem(stored, chip_rows) == wide, by_chip, 0.0), axis=0, keepdims=True)
        valid = table[entry : entry + 1, :] >= 0
        index[entry : entry + 1, :] = chip * PLACES + jnp.where(valid, place.astype(jnp.int32), 0)


def locate(chip_rows, entries, places, asked):
    return pl.pallas_call(
        functools.partial(locate_kernel, chip_rows, entries),
        in_specs=[VMEM, VMEM],
        out_specs=VMEM,
        out_shape=jax.ShapeDtypeStruct((8, asked.shape[0]), jnp.int32),
    )(places, asked)


def plan(chip_rows, entries, capacities, chip, asked):
    return pl.pallas_call(
        functools.partial(plan_kernel, chip_rows, entries, capacities),
        in_specs=[SMEM, VMEM],
        out_specs=(VMEM, VMEM, SMEM),
        out_shape=(
            jax.ShapeDtypeStruct((chip_rows, chip_rows), jnp.float32),
            jax.ShapeDtypeStruct((8, LANES), jnp.int32),
            jax.ShapeDtypeStruct((1,), jnp.int32),
        ),
    )(chip, asked)


def pick_kernel(core, rows, own, other, out, sems):
    images_dev = own.shape[0]
    capacity = out.shape[1]
    for slot in range(capacity):
        row = rows[0, slot]
        local = lax.rem(row, images_dev)
        is_own = lax.div(row, images_dev) == core[0]

        @pl.when(is_own)
        def _():
            pltpu.make_async_copy(own.at[local, core[0]], out.at[:, slot], sems.at[slot]).start()

        @pl.when(jnp.logical_not(is_own))
        def _():
            pltpu.make_async_copy(other.at[local, core[0]], out.at[:, slot], sems.at[slot]).start()

    for slot in range(capacity):
        pltpu.make_async_copy(other.at[0, 0], out.at[:, slot], sems.at[slot]).wait()


def pick(capacity, core, rows, own, other):
    _, _, chips, piece, width = other.shape
    return pl.pallas_call(
        pick_kernel,
        in_specs=[SMEM, SMEM, ANY, ANY],
        out_specs=VMEM,
        out_shape=jax.ShapeDtypeStruct((chips, capacity, piece, width), other.dtype),
        scratch_shapes=[pltpu.SemaphoreType.DMA((capacity,))],
        compiler_params=pltpu.CompilerParams(vmem_limit_bytes=24 * 1024 * 1024),
    )(core, rows, own, other)


def regroup_kernel(index, spread, out):
    groups, entries = out.shape[:2]

    def step(group, carry):
        for entry in range(entries):
            code = index[entry, group]
            out[group, entry] = spread[code >> PLACE_BITS, code & (PLACES - 1)]
        return carry

    lax.fori_loop(0, groups, step, 0, unroll=16)


def regroup(groups, entries, index, spread):
    return pl.pallas_call(
        regroup_kernel,
        in_specs=[SMEM, VMEM],
        out_specs=VMEM,
        out_shape=jax.ShapeDtypeStruct((groups, entries, *spread.shape[2:]), spread.dtype),
        compiler_params=pltpu.CompilerParams(vmem_limit_bytes=24 * 1024 * 1024),
    )(index, spread)


def score_kernel(image_rows, multiplier, pair, meta, maps, near_query, near_target, *refs):
    *earlier, products, rows, columns, scores, stats = refs
    for previous in earlier:
        columns[0:pair] = previous[...]
    chips, cores, entries, piece, width = maps.shape
    part = chips * piece
    slab = cores * part
    targets = ((maps, entries // 2 + pair), (near_target, 0))
    queries = ((maps, pair), (near_query, 0))

    @pl.when(pair < meta[1])
    def _():
        for row in range(2 * cores):
            target, entry = targets[row // cores]
            tokens = target[:, row % cores, entry].reshape(part, width)
            for column in range(2 * cores):
                query, entry = queries[column // cores]
                scores[row * part : (row + 1) * part, column * part : (column + 1) * part] = (
                    lax.dot_general(
                        tokens, query[:, column % cores, entry].reshape(part, width), (((1,), (1,)), ((), ())),
                        preferred_element_type=jnp.float32,
                    )
                    * multiplier
                )

        first_lane = lax.broadcasted_iota(jnp.int32, (64, LANES), 1) == 0

        def rows_step(index, carry):
            block = pl.ds(pl.multiple_of(index * 64, 64), 64)
            top = jnp.max(scores[block, :], axis=1, keepdims=True)
            powers = jnp.exp(scores[block, :] - top)
            products[block, :] = powers
            stats[block, :] = jnp.where(first_lane, top, jnp.sum(powers, axis=1, keepdims=True))
            return carry

        lax.fori_loop(0, 2 * slab // 64, rows_step, 0, unroll=16)
        for start in range(0, 2 * slab, LANES):
            columns[pair, :, start : start + LANES] = stats[start : start + LANES, :].T[0:8, :]

        bands = slab // IMG_W
        along = lax.broadcasted_iota(jnp.int32, (IMG_W, LANES), 0).astype(jnp.float32)
        coord_x = (2.0 * along + 1.0) / IMG_W - 1.0

        def lanes_step(index, carry):
            lanes = pl.ds(pl.multiple_of(index * LANES, LANES), LANES)
            top = jnp.max(scores[:, lanes], axis=0, keepdims=True)
            total = jnp.zeros((8, LANES), jnp.float32)
            weighted_y = jnp.zeros((8, LANES), jnp.float32)
            folded = jnp.zeros((IMG_W, LANES), jnp.float32)
            for band in range(2 * bands):
                block = slice(band * IMG_W, (band + 1) * IMG_W)
                powers = jnp.exp(scores[block, lanes] - top)
                products[block, lanes] *= powers
                folded += powers
                sums = jnp.sum(powers.reshape(IMG_W // 8, 8, LANES), axis=0)
                total += sums
                image_row = meta[2 + band // bands] * bands + band % bands
                weighted_y += sums * ((2.0 * image_row.astype(jnp.float32) + 1.0) / image_rows - 1.0)
            rows[0:1, lanes] = top
            rows[1:2, lanes] = jnp.sum(total, axis=0, keepdims=True)
            rows[2:3, lanes] = jnp.sum(folded * coord_x, axis=0, keepdims=True)
            rows[3:4, lanes] = jnp.sum(weighted_y, axis=0, keepdims=True)
            return carry

        lax.fori_loop(0, 2 * slab // LANES, lanes_step, 0, unroll=8)


def score(image_rows, multiplier, pair, meta, maps, near_query, near_target, earlier):
    chips, cores, _, piece, width = maps.shape
    tokens = 2 * chips * cores * piece
    return pl.pallas_call(
        functools.partial(score_kernel, image_rows, multiplier, pair),
        in_specs=[SMEM] + [VMEM] * (3 + len(earlier)),
        out_specs=[VMEM] * 3,
        out_shape=[
            jax.ShapeDtypeStruct((tokens, tokens), jnp.float32),
            jax.ShapeDtypeStruct((8, tokens), jnp.float32),
            jax.ShapeDtypeStruct((pair + 1, 8, tokens), jnp.float32),
        ],
        scratch_shapes=[pltpu.VMEM((tokens, tokens), jnp.float32), pltpu.VMEM((tokens, LANES), jnp.float32)],
        compiler_params=pltpu.CompilerParams(vmem_limit_bytes=20 * 1024 * 1024),
        cost_estimate=pl.CostEstimate(
            flops=2 * tokens * tokens * width, bytes_accessed=2 << 20, transcendentals=2 << 20
        ),
    )(meta, maps, near_query, near_target, *earlier)


def columns_kernel(multiplier, pair, meta, maps, near_query, near_target, *refs):
    *earlier, scores, powers, columns, stats = refs
    for previous in earlier:
        columns[0:pair] = previous[...]
    chips, cores, entries, piece, width = maps.shape
    part = chips * piece
    slab = cores * part
    targets = ((maps, entries // 2 + pair), (near_target, 0))
    queries = ((maps, pair), (near_query, 0))

    @pl.when(pair < meta[1])
    def _():
        for row in range(2 * cores):
            target, entry = targets[row // cores]
            tokens = target[:, row % cores, entry].reshape(part, width)
            for column in range(2 * cores):
                query, entry = queries[column // cores]
                scores[row * part : (row + 1) * part, column * part : (column + 1) * part] = (
                    lax.dot_general(
                        tokens, query[:, column % cores, entry].reshape(part, width), (((1,), (1,)), ((), ())),
                        preferred_element_type=jnp.float32,
                    )
                    * multiplier
                )

        first_lane = lax.broadcasted_iota(jnp.int32, (64, LANES), 1) == 0
        for start in range(0, 2 * slab, 64):
            block = slice(start, start + 64)
            top = jnp.max(scores[block, :], axis=1, keepdims=True)
            exponentials = jnp.exp(scores[block, :] - top)
            powers[block, :] = exponentials
            stats[block, :] = jnp.where(first_lane, top, jnp.sum(exponentials, axis=1, keepdims=True))
        for start in range(0, 2 * slab, LANES):
            columns[pair, :, start : start + LANES] = stats[start : start + LANES, :].T[0:8, :]


def score_columns(multiplier, pair, meta, maps, near_query, near_target, earlier):
    chips, cores, _, piece, width = maps.shape
    tokens = 2 * chips * cores * piece
    square = jax.ShapeDtypeStruct((tokens, tokens), jnp.float32)
    return pl.pallas_call(
        functools.partial(columns_kernel, multiplier, pair),
        in_specs=[SMEM] + [VMEM] * (3 + len(earlier)),
        out_specs=[VMEM] * 3,
        out_shape=[square, square, jax.ShapeDtypeStruct((pair + 1, 8, tokens), jnp.float32)],
        scratch_shapes=[pltpu.VMEM((tokens, LANES), jnp.float32)],
        compiler_params=pltpu.CompilerParams(vmem_limit_bytes=16 * 1024 * 1024),
        cost_estimate=pl.CostEstimate(
            flops=2 * tokens * tokens * width, bytes_accessed=2 << 20, transcendentals=1 << 20
        ),
    )(meta, maps, near_query, near_target, *earlier)


def rows_kernel(image_rows, pair, meta, scores, powers, products, rows):
    tokens = scores.shape[0]
    bands = tokens // (2 * IMG_W)

    @pl.when(pair < meta[1])
    def _():
        along = lax.broadcasted_iota(jnp.int32, (IMG_W, LANES), 0).astype(jnp.float32)
        coord_x = (2.0 * along + 1.0) / IMG_W - 1.0
        for start in range(0, tokens, LANES):
            lanes = slice(start, start + LANES)
            top = jnp.max(scores[:, lanes], axis=0, keepdims=True)
            total = jnp.zeros((8, LANES), jnp.float32)
            weighted_y = jnp.zeros((8, LANES), jnp.float32)
            folded = jnp.zeros((IMG_W, LANES), jnp.float32)
            for band in range(2 * bands):
                block = slice(band * IMG_W, (band + 1) * IMG_W)
                exponentials = jnp.exp(scores[block, lanes] - top)
                products[block, lanes] = powers[block, lanes] * exponentials
                folded += exponentials
                sums = jnp.sum(exponentials.reshape(IMG_W // 8, 8, LANES), axis=0)
                total += sums
                image_row = meta[2 + band // bands] * bands + band % bands
                weighted_y += sums * ((2.0 * image_row.astype(jnp.float32) + 1.0) / image_rows - 1.0)
            rows[0:1, lanes] = top
            rows[1:2, lanes] = jnp.sum(total, axis=0, keepdims=True)
            rows[2:3, lanes] = jnp.sum(folded * coord_x, axis=0, keepdims=True)
            rows[3:4, lanes] = jnp.sum(weighted_y, axis=0, keepdims=True)


def score_rows(image_rows, pair, meta, scores, powers):
    tokens = scores.shape[0]
    return pl.pallas_call(
        functools.partial(rows_kernel, image_rows, pair),
        in_specs=[SMEM] + [VMEM] * 2,
        out_specs=[VMEM] * 2,
        out_shape=[
            jax.ShapeDtypeStruct((tokens, tokens), jnp.float32),
            jax.ShapeDtypeStruct((8, tokens), jnp.float32),
        ],
        compiler_params=pltpu.CompilerParams(vmem_limit_bytes=16 * 1024 * 1024),
        cost_estimate=pl.CostEstimate(flops=10 << 20, bytes_accessed=8 << 20, transcendentals=1 << 20),
    )(meta, scores, powers)


def mutual_kernel(pairs, meta, *refs):
    products, rows = refs[:pairs], refs[pairs : 2 * pairs]
    columns, others, kept, sent, weights = refs[2 * pairs :]
    tokens = weights.shape[0]
    slab = tokens // 2
    for pair in range(pairs):

        @pl.when(pair < meta[1])
        def _():
            for start in range(0, tokens, LANES):
                here = slice(start, start + LANES)
                there = slice((start + slab) % tokens, (start + slab) % tokens + LANES)
                top = columns[pair, 0:1, here]
                other_top = others[pair, 0:1, there]
                highest = jnp.maximum(top, other_top)
                scale = jnp.exp(top - highest)
                total = columns[pair, 1:2, here] * scale + others[pair, 1:2, there] * jnp.exp(other_top - highest)
                weights[here, :] = jnp.broadcast_to(scale / total, (LANES, LANES)).T

            for half, out in enumerate((kept, sent)):
                out[pair, 0:4, :] = rows[pair][0:4, half * slab : (half + 1) * slab]
                for start in range(0, slab, LANES):
                    lanes = slice(half * slab + start, half * slab + start + LANES)
                    mutual = jnp.zeros((64, LANES), jnp.float32)
                    for row in range(0, tokens, 64):
                        mutual += products[pair][row : row + 64, lanes] * weights[row : row + 64, :]
                    out[pair, 4:5, start : start + LANES] = jnp.sum(mutual, axis=0, keepdims=True)


def mutual(meta, products, rows, columns, others):
    pairs = len(products)
    tokens = products[0].shape[0]
    shape = jax.ShapeDtypeStruct((pairs, 8, tokens // 2), jnp.float32)
    return pl.pallas_call(
        functools.partial(mutual_kernel, pairs),
        in_specs=[SMEM] + [VMEM] * (2 * pairs + 2),
        out_specs=[VMEM] * 2,
        out_shape=[shape] * 2,
        scratch_shapes=[pltpu.VMEM((tokens, LANES), jnp.float32)],
        compiler_params=pltpu.CompilerParams(vmem_limit_bytes=20 * 1024 * 1024),
    )(meta, *products, *rows, columns, others)


def shards(picture_descriptors, image_slot, group_images, pair_target, pair_count):
    chips = lax.axis_size("chip")
    cores = lax.axis_size("core")
    quads = lax.axis_size("quad")
    groups = chips * cores
    chip = lax.axis_index("chip").astype(jnp.int32)
    core = lax.axis_index("core").astype(jnp.int32)
    quad = lax.axis_index("quad").astype(jnp.int32)
    images_dev, slab, width = picture_descriptors.shape
    pairs = pair_target.shape[0]
    chip_rows = images_dev * cores
    image_rows = slab * quads // IMG_W
    multiplier = 1.0 / (width * SHARPNESS_DIVISOR)

    def all_pairs(array):
        return lax.all_to_all(array, ("chip", "core"), split_axis=0, concat_axis=0, tiled=True)

    traded = lax.ppermute(picture_descriptors, "core", [(i, (i + 1) % cores) for i in range(cores)])

    asked = all_pairs(announce(groups, image_slot, group_images, pair_target, pair_count))

    capacities = [size for size in CAPACITIES if size < chip_rows] + [chip_rows]
    asked = asked.reshape(groups, LANES)
    places, listed, branch = plan(chip_rows, 2 * pairs, capacities, chip[None], asked)
    halves = (images_dev, cores, chips, slab // groups, width)

    def exchange(capacity, operands):
        own, other, rows, places, asked = operands
        pieces = pick(capacity, core[None], rows, own, other)
        spread = lax.all_to_all(pieces, "chip", split_axis=0, concat_axis=0, tiled=True)
        return regroup(groups, 2 * pairs, locate(chip_rows, 2 * pairs, places, asked), spread)

    pieces = lax.switch(
        branch[0],
        [functools.partial(exchange, size) for size in capacities],
        (picture_descriptors.reshape(halves), traded.reshape(halves), listed, places, asked),
    )
    maps = all_pairs(pieces).reshape(chips, cores, *pieces.shape[1:])

    def trade(array, flip):
        return lax.ppermute(array, "quad", [(i, i ^ flip) for i in range(quads)])

    query_flip, target_flip = 1, quads - 1
    meta = jnp.stack([quad, pair_count[0], quad, quad ^ target_flip])
    products, rows, columns = [], [], ()
    for pair in range(pairs):
        near_query = trade(maps[:, :, pair : pair + 1], query_flip)
        near_target = trade(maps[:, :, pairs + pair : pairs + pair + 1], target_flip)
        if pair < pairs - 1:
            product, row, column = score(image_rows, multiplier, pair, meta, maps, near_query, near_target, columns)
        else:
            scores, powers, column = score_columns(multiplier, pair, meta, maps, near_query, near_target, columns)
            others = trade(column, target_flip)
            product, row = score_rows(image_rows, pair, meta, scores, powers)
        products.append(product)
        rows.append(row)
        columns = (column,)
    kept, sent = mutual(meta, products, rows, columns[0], others)
    partial = jnp.stack([kept, trade(sent, query_flip)])
    top = partial[:, :, 0]
    weight = jnp.exp(top - jnp.max(top, axis=0, keepdims=True))
    total = jnp.sum(partial[:, :, 1] * weight, axis=0)
    fields = [jnp.sum(partial[:, :, 2 + field] * weight, axis=0) / total for field in range(3)]
    in_use = jnp.arange(pairs, dtype=jnp.int32) < pair_count[0]
    return jnp.where(in_use[None, :, None], jnp.stack(fields), 0.0).transpose(1, 0, 2)


def solution(mesh):
    pair_axis = ("chip", "core")
    split = Mesh(mesh.devices.reshape(-1, CORES, mesh.devices.shape[-1]), (*pair_axis, "quad"))
    return jax.shard_map(
        shards,
        mesh=split,
        in_specs=(P(pair_axis, "quad", None), P(), P(pair_axis), P(pair_axis), P(pair_axis)),
        out_specs=P(pair_axis, None, "quad"),
        check_vma=False,
    )
```

```python
import functools

import jax
import jax.numpy as jnp
from jax import lax
from jax.experimental import pallas as pl
from jax.experimental.pallas import tpu as pltpu
from jax.sharding import Mesh
from jax.sharding import PartitionSpec as P

IMG_W = 64
TGT_G = 8
SHARPNESS_DIVISOR = 0.1
LANES = 128
CORES = 2
PLACE_BITS = 6
PLACES = 1 << PLACE_BITS
CAPACITIES = (6, 7, 8, 9, 10, 11, 12, 16)
ANY = pl.BlockSpec(memory_space=pl.ANY)
SMEM = pl.BlockSpec(memory_space=pltpu.SMEM)
VMEM = pl.BlockSpec(memory_space=pltpu.VMEM)


def announce_kernel(pairs, image_slot, group_images, pair_target, pair_count, out):
    lane = lax.broadcasted_iota(jnp.int32, out.shape, 2)
    message = jnp.full(out.shape, -1, jnp.int32)
    for entry in range(2 * pairs):
        pair = entry % pairs
        member = TGT_G + pair if entry < pairs else pair_target[pair]
        stored = jnp.where(pair < pair_count[0], image_slot[group_images[member]], -1)
        message = jnp.where(lane == entry, stored, message)
    out[...] = message


def announce(groups, image_slot, group_images, pair_target, pair_count):
    return pl.pallas_call(
        functools.partial(announce_kernel, pair_target.shape[0]),
        in_specs=[SMEM] * 4,
        out_specs=VMEM,
        out_shape=jax.ShapeDtypeStruct((groups, 1, LANES), jnp.int32),
    )(image_slot, group_images, pair_target, pair_count)


def plan_kernel(chip_rows, entries, capacities, chip, asked, places, rows, branch):
    groups = asked.shape[0]
    table = asked[...].T
    chips_of, rows_of, stored_of = [], [], []
    wide = lax.broadcasted_iota(jnp.int32, (chip_rows, groups), 0)
    count = jnp.zeros((chip_rows, chip_rows), jnp.float32)
    for entry in range(entries):
        stored = table[entry : entry + 1, :]
        valid = jnp.where(stored >= 0, 1.0, 0.0)
        stored_of.append(jnp.maximum(stored, 0))
        chips_of.append(jnp.where(lax.div(stored_of[-1], chip_rows) == wide, valid, 0.0))
        rows_of.append(jnp.where(lax.rem(stored_of[-1], chip_rows) == wide, 1.0, 0.0))
        count += lax.dot_general(
            rows_of[-1], chips_of[-1], (((1,), (1,)), ((), ())), preferred_element_type=jnp.float32
        )
    flags = jnp.where(count > 0.0, 1.0, 0.0)
    first = lax.broadcasted_iota(jnp.int32, (chip_rows, chip_rows), 0)
    second = lax.broadcasted_iota(jnp.int32, (chip_rows, chip_rows), 1)
    earlier = jnp.dot(jnp.where(second < first, 1.0, 0.0), flags, preferred_element_type=jnp.float32)
    most = jnp.max(earlier + flags)
    choice = jnp.int32(0)
    for capacity in capacities[:-1]:
        choice += jnp.where(most > capacity, 1, 0)
    branch[0] = choice

    here = second == chip[0]
    my_flag = jnp.max(jnp.where(here, flags, 0.0), axis=1, keepdims=True)
    my_place = jnp.max(jnp.where(here, earlier, 0.0), axis=1, keepdims=True)
    slot = lax.broadcasted_iota(jnp.int32, (chip_rows, LANES), 1).astype(jnp.float32)
    row = lax.broadcasted_iota(jnp.int32, (chip_rows, LANES), 0).astype(jnp.float32)
    chosen = jnp.where((my_flag > 0.0) & (my_place == slot), row, 0.0)
    rows[...] = jnp.broadcast_to(jnp.sum(chosen, axis=0, keepdims=True), rows.shape).astype(jnp.int32)

    places[...] = earlier


def locate_kernel(chip_rows, entries, places, asked, index):
    groups = asked.shape[0]
    table = asked[...].T
    wide = lax.broadcasted_iota(jnp.int32, (chip_rows, groups), 0)
    for entry in range(entries):
        stored = jnp.maximum(table[entry : entry + 1, :], 0)
        chip = lax.div(stored, chip_rows)
        by_chip = jnp.dot(places[...], jnp.where(chip == wide, 1.0, 0.0), preferred_element_type=jnp.float32)
        place = jnp.sum(jnp.where(lax.rem(stored, chip_rows) == wide, by_chip, 0.0), axis=0, keepdims=True)
        valid = table[entry : entry + 1, :] >= 0
        index[entry : entry + 1, :] = chip * PLACES + jnp.where(valid, place.astype(jnp.int32), 0)


def locate(chip_rows, entries, places, asked):
    return pl.pallas_call(
        functools.partial(locate_kernel, chip_rows, entries),
        in_specs=[VMEM, VMEM],
        out_specs=VMEM,
        out_shape=jax.ShapeDtypeStruct((8, asked.shape[0]), jnp.int32),
    )(places, asked)


def plan(chip_rows, entries, capacities, chip, asked):
    return pl.pallas_call(
        functools.partial(plan_kernel, chip_rows, entries, capacities),
        in_specs=[SMEM, VMEM],
        out_specs=(VMEM, VMEM, SMEM),
        out_shape=(
            jax.ShapeDtypeStruct((chip_rows, chip_rows), jnp.float32),
            jax.ShapeDtypeStruct((8, LANES), jnp.int32),
            jax.ShapeDtypeStruct((1,), jnp.int32),
        ),
    )(chip, asked)


def pick_kernel(core, rows, own, other, out, sems):
    images_dev = own.shape[0]
    capacity = out.shape[1]
    for slot in range(capacity):
        row = rows[0, slot]
        local = lax.rem(row, images_dev)
        is_own = lax.div(row, images_dev) == core[0]

        @pl.when(is_own)
        def _():
            pltpu.make_async_copy(own.at[local, core[0]], out.at[:, slot], sems.at[slot]).start()

        @pl.when(jnp.logical_not(is_own))
        def _():
            pltpu.make_async_copy(other.at[local, core[0]], out.at[:, slot], sems.at[slot]).start()

    for slot in range(capacity):
        pltpu.make_async_copy(other.at[0, 0], out.at[:, slot], sems.at[slot]).wait()


def pick(capacity, core, rows, own, other):
    _, _, chips, piece, width = other.shape
    return pl.pallas_call(
        pick_kernel,
        in_specs=[SMEM, SMEM, ANY, ANY],
        out_specs=VMEM,
        out_shape=jax.ShapeDtypeStruct((chips, capacity, piece, width), other.dtype),
        scratch_shapes=[pltpu.SemaphoreType.DMA((capacity,))],
        compiler_params=pltpu.CompilerParams(vmem_limit_bytes=24 * 1024 * 1024),
    )(core, rows, own, other)


def regroup_kernel(located, spread, out, index, sem):
    groups, entries = out.shape[:2]
    copy = pltpu.make_async_copy(located, index, sem)
    copy.start()
    copy.wait()

    def step(group, carry):
        for entry in range(entries):
            code = index[entry, group]
            out[group, entry] = spread[code >> PLACE_BITS, code & (PLACES - 1)]
        return carry

    lax.fori_loop(0, groups, step, 0, unroll=16)


def regroup(groups, entries, index, spread):
    return pl.pallas_call(
        regroup_kernel,
        in_specs=[ANY, VMEM],
        out_specs=VMEM,
        out_shape=jax.ShapeDtypeStruct((groups, entries, *spread.shape[2:]), spread.dtype),
        scratch_shapes=[pltpu.SMEM(index.shape, jnp.int32), pltpu.SemaphoreType.DMA(())],
        compiler_params=pltpu.CompilerParams(vmem_limit_bytes=24 * 1024 * 1024),
    )(index, spread)


def score_kernel(image_rows, multiplier, pair, meta, maps, near_query, near_target, *refs):
    *earlier, products, rows, columns, scores, stats = refs
    for previous in earlier:
        columns[0:pair] = previous[...]
    chips, cores, entries, piece, width = maps.shape
    part = chips * piece
    slab = cores * part
    targets = ((maps, entries // 2 + pair), (near_target, 0))
    queries = ((maps, pair), (near_query, 0))

    @pl.when(pair < meta[1])
    def _():
        for row in range(2 * cores):
            target, entry = targets[row // cores]
            tokens = target[:, row % cores, entry].reshape(part, width)
            for column in range(2 * cores):
                query, entry = queries[column // cores]
                scores[row * part : (row + 1) * part, column * part : (column + 1) * part] = (
                    lax.dot_general(
                        tokens, query[:, column % cores, entry].reshape(part, width), (((1,), (1,)), ((), ())),
                        preferred_element_type=jnp.float32,
                    )
                    * multiplier
                )

        first_lane = lax.broadcasted_iota(jnp.int32, (64, LANES), 1) == 0

        def rows_step(index, carry):
            block = pl.ds(pl.multiple_of(index * 64, 64), 64)
            top = jnp.max(scores[block, :], axis=1, keepdims=True)
            powers = jnp.exp(scores[block, :] - top)
            products[block, :] = powers
            stats[block, :] = jnp.where(first_lane, top, jnp.sum(powers, axis=1, keepdims=True))
            return carry

        lax.fori_loop(0, 2 * slab // 64, rows_step, 0, unroll=16)
        for start in range(0, 2 * slab, LANES):
            columns[pair, :, start : start + LANES] = stats[start : start + LANES, :].T[0:8, :]

        bands = slab // IMG_W
        along = lax.broadcasted_iota(jnp.int32, (IMG_W, LANES), 0).astype(jnp.float32)
        coord_x = (2.0 * along + 1.0) / IMG_W - 1.0

        def lanes_step(index, carry):
            lanes = pl.ds(pl.multiple_of(index * LANES, LANES), LANES)
            top = jnp.max(scores[:, lanes], axis=0, keepdims=True)
            total = jnp.zeros((8, LANES), jnp.float32)
            weighted_y = jnp.zeros((8, LANES), jnp.float32)
            folded = jnp.zeros((IMG_W, LANES), jnp.float32)
            for band in range(2 * bands):
                block = slice(band * IMG_W, (band + 1) * IMG_W)
                powers = jnp.exp(scores[block, lanes] - top)
                products[block, lanes] *= powers
                folded += powers
                sums = jnp.sum(powers.reshape(IMG_W // 8, 8, LANES), axis=0)
                total += sums
                image_row = meta[2 + band // bands] * bands + band % bands
                weighted_y += sums * ((2.0 * image_row.astype(jnp.float32) + 1.0) / image_rows - 1.0)
            rows[0:1, lanes] = top
            rows[1:2, lanes] = jnp.sum(total, axis=0, keepdims=True)
            rows[2:3, lanes] = jnp.sum(folded * coord_x, axis=0, keepdims=True)
            rows[3:4, lanes] = jnp.sum(weighted_y, axis=0, keepdims=True)
            return carry

        lax.fori_loop(0, 2 * slab // LANES, lanes_step, 0, unroll=8)


def score(image_rows, multiplier, pair, meta, maps, near_query, near_target, earlier):
    chips, cores, _, piece, width = maps.shape
    tokens = 2 * chips * cores * piece
    return pl.pallas_call(
        functools.partial(score_kernel, image_rows, multiplier, pair),
        in_specs=[SMEM] + [VMEM] * (3 + len(earlier)),
        out_specs=[VMEM] * 3,
        out_shape=[
            jax.ShapeDtypeStruct((tokens, tokens), jnp.float32),
            jax.ShapeDtypeStruct((8, tokens), jnp.float32),
            jax.ShapeDtypeStruct((pair + 1, 8, tokens), jnp.float32),
        ],
        scratch_shapes=[pltpu.VMEM((tokens, tokens), jnp.float32), pltpu.VMEM((tokens, LANES), jnp.float32)],
        compiler_params=pltpu.CompilerParams(vmem_limit_bytes=20 * 1024 * 1024),
        cost_estimate=pl.CostEstimate(
            flops=2 * tokens * tokens * width, bytes_accessed=2 << 20, transcendentals=2 << 20
        ),
    )(meta, maps, near_query, near_target, *earlier)


def columns_kernel(multiplier, pair, meta, maps, near_query, near_target, *refs):
    *earlier, scores, powers, columns, stats = refs
    for previous in earlier:
        columns[0:pair] = previous[...]
    chips, cores, entries, piece, width = maps.shape
    part = chips * piece
    slab = cores * part
    targets = ((maps, entries // 2 + pair), (near_target, 0))
    queries = ((maps, pair), (near_query, 0))

    @pl.when(pair < meta[1])
    def _():
        for row in range(2 * cores):
            target, entry = targets[row // cores]
            tokens = target[:, row % cores, entry].reshape(part, width)
            for column in range(2 * cores):
                query, entry = queries[column // cores]
                scores[row * part : (row + 1) * part, column * part : (column + 1) * part] = (
                    lax.dot_general(
                        tokens, query[:, column % cores, entry].reshape(part, width), (((1,), (1,)), ((), ())),
                        preferred_element_type=jnp.float32,
                    )
                    * multiplier
                )

        first_lane = lax.broadcasted_iota(jnp.int32, (64, LANES), 1) == 0
        for start in range(0, 2 * slab, 64):
            block = slice(start, start + 64)
            top = jnp.max(scores[block, :], axis=1, keepdims=True)
            exponentials = jnp.exp(scores[block, :] - top)
            powers[block, :] = exponentials
            stats[block, :] = jnp.where(first_lane, top, jnp.sum(exponentials, axis=1, keepdims=True))
        for start in range(0, 2 * slab, LANES):
            columns[pair, :, start : start + LANES] = stats[start : start + LANES, :].T[0:8, :]


def score_columns(multiplier, pair, meta, maps, near_query, near_target, earlier):
    chips, cores, _, piece, width = maps.shape
    tokens = 2 * chips * cores * piece
    square = jax.ShapeDtypeStruct((tokens, tokens), jnp.float32)
    return pl.pallas_call(
        functools.partial(columns_kernel, multiplier, pair),
        in_specs=[SMEM] + [VMEM] * (3 + len(earlier)),
        out_specs=[VMEM] * 3,
        out_shape=[square, square, jax.ShapeDtypeStruct((pair + 1, 8, tokens), jnp.float32)],
        scratch_shapes=[pltpu.VMEM((tokens, LANES), jnp.float32)],
        compiler_params=pltpu.CompilerParams(vmem_limit_bytes=16 * 1024 * 1024),
        cost_estimate=pl.CostEstimate(
            flops=2 * tokens * tokens * width, bytes_accessed=2 << 20, transcendentals=1 << 20
        ),
    )(meta, maps, near_query, near_target, *earlier)


def rows_kernel(image_rows, pair, meta, scores, powers, products, rows):
    tokens = scores.shape[0]
    bands = tokens // (2 * IMG_W)

    @pl.when(pair < meta[1])
    def _():
        along = lax.broadcasted_iota(jnp.int32, (IMG_W, LANES), 0).astype(jnp.float32)
        coord_x = (2.0 * along + 1.0) / IMG_W - 1.0
        for start in range(0, tokens, LANES):
            lanes = slice(start, start + LANES)
            top = jnp.max(scores[:, lanes], axis=0, keepdims=True)
            total = jnp.zeros((8, LANES), jnp.float32)
            weighted_y = jnp.zeros((8, LANES), jnp.float32)
            folded = jnp.zeros((IMG_W, LANES), jnp.float32)
            for band in range(2 * bands):
                block = slice(band * IMG_W, (band + 1) * IMG_W)
                exponentials = jnp.exp(scores[block, lanes] - top)
                products[block, lanes] = powers[block, lanes] * exponentials
                folded += exponentials
                sums = jnp.sum(exponentials.reshape(IMG_W // 8, 8, LANES), axis=0)
                total += sums
                image_row = meta[2 + band // bands] * bands + band % bands
                weighted_y += sums * ((2.0 * image_row.astype(jnp.float32) + 1.0) / image_rows - 1.0)
            rows[0:1, lanes] = top
            rows[1:2, lanes] = jnp.sum(total, axis=0, keepdims=True)
            rows[2:3, lanes] = jnp.sum(folded * coord_x, axis=0, keepdims=True)
            rows[3:4, lanes] = jnp.sum(weighted_y, axis=0, keepdims=True)


def score_rows(image_rows, pair, meta, scores, powers):
    tokens = scores.shape[0]
    return pl.pallas_call(
        functools.partial(rows_kernel, image_rows, pair),
        in_specs=[SMEM] + [VMEM] * 2,
        out_specs=[VMEM] * 2,
        out_shape=[
            jax.ShapeDtypeStruct((tokens, tokens), jnp.float32),
            jax.ShapeDtypeStruct((8, tokens), jnp.float32),
        ],
        compiler_params=pltpu.CompilerParams(vmem_limit_bytes=16 * 1024 * 1024),
        cost_estimate=pl.CostEstimate(flops=10 << 20, bytes_accessed=8 << 20, transcendentals=1 << 20),
    )(meta, scores, powers)


def mutual_kernel(pairs, meta, *refs):
    products, rows = refs[:pairs], refs[pairs : 2 * pairs]
    columns, others, kept, sent, weights = refs[2 * pairs :]
    tokens = weights.shape[0]
    slab = tokens // 2
    for pair in range(pairs):

        @pl.when(pair < meta[1])
        def _():
            for start in range(0, tokens, LANES):
                here = slice(start, start + LANES)
                there = slice((start + slab) % tokens, (start + slab) % tokens + LANES)
                top = columns[pair, 0:1, here]
                other_top = others[pair, 0:1, there]
                highest = jnp.maximum(top, other_top)
                scale = jnp.exp(top - highest)
                total = columns[pair, 1:2, here] * scale + others[pair, 1:2, there] * jnp.exp(other_top - highest)
                weights[here, :] = jnp.broadcast_to(scale / total, (LANES, LANES)).T

            for half, out in enumerate((kept, sent)):
                out[pair, 0:4, :] = rows[pair][0:4, half * slab : (half + 1) * slab]
                for start in range(0, slab, LANES):
                    lanes = slice(half * slab + start, half * slab + start + LANES)
                    mutual = jnp.zeros((64, LANES), jnp.float32)
                    for row in range(0, tokens, 64):
                        mutual += products[pair][row : row + 64, lanes] * weights[row : row + 64, :]
                    out[pair, 4:5, start : start + LANES] = jnp.sum(mutual, axis=0, keepdims=True)


def mutual(meta, products, rows, columns, others):
    pairs = len(products)
    tokens = products[0].shape[0]
    shape = jax.ShapeDtypeStruct((pairs, 8, tokens // 2), jnp.float32)
    return pl.pallas_call(
        functools.partial(mutual_kernel, pairs),
        in_specs=[SMEM] + [VMEM] * (2 * pairs + 2),
        out_specs=[VMEM] * 2,
        out_shape=[shape] * 2,
        scratch_shapes=[pltpu.VMEM((tokens, LANES), jnp.float32)],
        compiler_params=pltpu.CompilerParams(vmem_limit_bytes=20 * 1024 * 1024),
    )(meta, *products, *rows, columns, others)


def shards(picture_descriptors, image_slot, group_images, pair_target, pair_count):
    chips = lax.axis_size("chip")
    cores = lax.axis_size("core")
    quads = lax.axis_size("quad")
    groups = chips * cores
    chip = lax.axis_index("chip").astype(jnp.int32)
    core = lax.axis_index("core").astype(jnp.int32)
    quad = lax.axis_index("quad").astype(jnp.int32)
    images_dev, slab, width = picture_descriptors.shape
    pairs = pair_target.shape[0]
    chip_rows = images_dev * cores
    image_rows = slab * quads // IMG_W
    multiplier = 1.0 / (width * SHARPNESS_DIVISOR)

    def all_pairs(array):
        return lax.all_to_all(array, ("chip", "core"), split_axis=0, concat_axis=0, tiled=True)

    traded = lax.ppermute(picture_descriptors, "core", [(i, (i + 1) % cores) for i in range(cores)])

    asked = all_pairs(announce(groups, image_slot, group_images, pair_target, pair_count))

    capacities = [size for size in CAPACITIES if size < chip_rows] + [chip_rows]
    asked = asked.reshape(groups, LANES)
    places, listed, branch = plan(chip_rows, 2 * pairs, capacities, chip[None], asked)
    halves = (images_dev, cores, chips, slab // groups, width)

    def exchange(capacity, operands):
        own, other, rows, places, asked = operands
        pieces = pick(capacity, core[None], rows, own, other)
        spread = lax.all_to_all(pieces, "chip", split_axis=0, concat_axis=0, tiled=True)
        return regroup(groups, 2 * pairs, locate(chip_rows, 2 * pairs, places, asked), spread)

    pieces = lax.switch(
        branch[0],
        [functools.partial(exchange, size) for size in capacities],
        (picture_descriptors.reshape(halves), traded.reshape(halves), listed, places, asked),
    )
    maps = all_pairs(pieces).reshape(chips, cores, *pieces.shape[1:])

    def trade(array, flip):
        return lax.ppermute(array, "quad", [(i, i ^ flip) for i in range(quads)])

    query_flip, target_flip = 1, quads - 1
    meta = jnp.stack([quad, pair_count[0], quad, quad ^ target_flip])
    products, rows, columns = [], [], ()
    for pair in range(pairs):
        near_query = trade(maps[:, :, pair : pair + 1], query_flip)
        near_target = trade(maps[:, :, pairs + pair : pairs + pair + 1], target_flip)
        if pair < pairs - 1:
            product, row, column = score(image_rows, multiplier, pair, meta, maps, near_query, near_target, columns)
        else:
            scores, powers, column = score_columns(multiplier, pair, meta, maps, near_query, near_target, columns)
            others = trade(column, target_flip)
            product, row = score_rows(image_rows, pair, meta, scores, powers)
        products.append(product)
        rows.append(row)
        columns = (column,)
    kept, sent = mutual(meta, products, rows, columns[0], others)
    partial = jnp.stack([kept, trade(sent, query_flip)])
    top = partial[:, :, 0]
    weight = jnp.exp(top - jnp.max(top, axis=0, keepdims=True))
    total = jnp.sum(partial[:, :, 1] * weight, axis=0)
    fields = [jnp.sum(partial[:, :, 2 + field] * weight, axis=0) / total for field in range(3)]
    in_use = jnp.arange(pairs, dtype=jnp.int32) < pair_count[0]
    return jnp.where(in_use[None, :, None], jnp.stack(fields), 0.0).transpose(1, 0, 2)


def solution(mesh):
    pair_axis = ("chip", "core")
    split = Mesh(mesh.devices.reshape(-1, CORES, mesh.devices.shape[-1]), (*pair_axis, "quad"))
    return jax.shard_map(
        shards,
        mesh=split,
        in_specs=(P(pair_axis, "quad", None), P(), P(pair_axis), P(pair_axis), P(pair_axis)),
        out_specs=P(pair_axis, None, "quad"),
        check_vma=False,
    )
```
